32 devices in a mesh: outer: 8 (over z, x), inner: 4 (over y, core).
Axes of the slice: x: 2, y: 2, z: 4, core: 2. Of those that a mesh axis runs over, the one named last changes fastest.
Arguments:
- queries: bfloat16 [32768, 1024], P(('outer', 'inner')), may hold values from -6 to 6
- keys: bfloat16 [32768, 1024], P(('outer', 'inner')), may hold values from -6 to 6
- values: bfloat16 [32768, 1024], P(('outer', 'inner')), may hold values from -6 to 6
- norm_gain: float32 [1024], replicated, may hold values from 0.1 to 1.9
- out_weight: bfloat16 [1024, 2048], replicated, may hold values from -0.1875 to 0.1875
Outputs:
- mixed: bfloat16 [32768, 2048], P(('outer', 'inner'))
The draws below stay inside these ranges and needn't reach their ends.
All inputs are finite; a program needn't handle non-finite values.
Results may differ from the reference program's by a relative error of at most 0.0058.
Values sent between devices are 32-bit elements; how exact they have to be, the bound alone decides.
A program may use at most 320 MiB of HBM per device.

```python
import jax
import jax.numpy as jnp
from jax import lax

D = 2048
H = 8
DH = 128
C = 128
TOK_DEV = 1024
HD = 1024
TOKENS = 32768


def level_of(rng, shape, split, low, high):
    level, own = 1.0, jax.random.fold_in(rng, 6)
    for dim, parts in split:
        heights = jnp.exp(jax.random.uniform(jax.random.fold_in(own, dim), (parts,), jnp.float32, low / len(split), high / len(split)))
        level = level * jnp.repeat(heights, shape[dim] // parts).reshape([-1 if axis == dim else 1 for axis in range(len(shape))])
    return level


def bell_draw(own_key, extent, deviation, bound, pieces=(), kind=jnp.bfloat16):
    result = jax.random.normal(own_key, extent, jnp.float32) * deviation
    if len(pieces) > 0:
        result = level_of(own_key, extent, pieces, -0.22, 0.18) * result
    return jnp.clip(result, min=-bound, max=bound).astype(kind)


def setup_inputs(seed: int = 0) -> dict:
    arg_keys = jax.random.split(jax.random.key(seed), 6)
    return {
        "queries": bell_draw(arg_keys[0], (TOKENS, HD), 1.0, 6.0, ((0, 32),)),
        "keys": bell_draw(arg_keys[1], (TOKENS, HD), 1.0, 6.0, ((0, 32),)),
        "values": bell_draw(arg_keys[2], (TOKENS, HD), 1.0, 6.0, ((0, 32),)),
        "norm_gain": jnp.clip(1.0 + 0.18 * jax.random.normal(arg_keys[3], (HD,), jnp.float32), 0.1, 1.9),
        "out_weight": bell_draw(arg_keys[4], (HD, D), HD ** -0.5, 0.1875),
    }


def block_step(carried, inputs):
    query_rows, key_rows, value_rows, norm_gain, out_weight = inputs
    blocks = TOK_DEV // C
    query_blocks = query_rows.reshape(blocks, C, H, DH).astype(jnp.float32)
    key_blocks = key_rows.reshape(blocks, C, H, DH).astype(jnp.float32)
    value_blocks = value_rows.reshape(blocks, C, H, DH).astype(jnp.float32)
    states = jnp.einsum('nchd,nche->nhde', key_blocks, value_blocks)
    running = jnp.cumsum(states, axis=0)
    within = jnp.concatenate([jnp.zeros_like(carried)[None], running[:-1]], axis=0)
    prefix_low = (carried[None] + within).astype(jnp.bfloat16)
    scores = jnp.einsum('nchd,nshd->nhcs', query_blocks, key_blocks)
    causal = jnp.arange(C)[:, None] >= jnp.arange(C)[None, :]
    weights = jnp.where(causal[None, None], scores, 0.0).astype(jnp.bfloat16)
    inside = jnp.einsum('nhcs,nshd->nchd', weights.astype(jnp.float32), value_blocks)
    carried_term = jnp.einsum('nchd,nhde->nche', query_blocks, prefix_low.astype(jnp.float32))
    attended = inside + carried_term
    mean_square = lax.optimization_barrier(jnp.mean(attended * attended, axis=-1, keepdims=True))
    normed = attended * lax.rsqrt(mean_square + 1e-06) * norm_gain.reshape(H, DH)
    normed = normed.astype(jnp.bfloat16).reshape(TOK_DEV, H * DH)
    mixed = jnp.dot(normed, out_weight, preferred_element_type=jnp.float32).astype(jnp.bfloat16)
    return (carried + lax.optimization_barrier(jnp.sum(states, axis=0)), mixed)

def reference(queries, keys, values, norm_gain, out_weight):
    count = TOKENS // TOK_DEV
    width = H * DH
    query_all = queries.reshape(count, TOK_DEV, width)
    key_all = keys.reshape(count, TOK_DEV, width)
    value_all = values.reshape(count, TOK_DEV, width)

    def step(carried, trio):
        return block_step(carried, (trio[0], trio[1], trio[2], norm_gain, out_weight))
    start_state = jnp.zeros((H, DH, DH), jnp.float32)
    final_state, mixed = lax.scan(step, start_state, (query_all, key_all, value_all))
    return mixed.reshape(TOKENS, D)
```

```python
import functools

import jax
import jax.numpy as jnp
from jax import lax
from jax.experimental import pallas as pl
from jax.experimental.pallas import tpu as pltpu
from jax.sharding import PartitionSpec as P

H = 8
DH = 128
PAIRS = H // 2
PW = 2 * DH
CHUNK = 256
ROWS = 256
F32 = jnp.float32
BF16 = jnp.bfloat16
MESH = pl.DeviceIdType.MESH
ORDER = (1, 3, 2, 0)


def scan_kernel(
    n_outer, n_inner, q_hbm, k_hbm, v_hbm, s_ref, pre_hbm,
    q, k, v, pre, local, pair_buf, chip, up_buf, zs, zb, zx, down_src, down_buf, fwd, pd,
    load_sem, store_sem, pair_send, pair_recv, up_send, up_recv, z_send, z_recv,
    down_send, down_recv, fwd_send, fwd_recv,
):
    tok = q.shape[0]
    groups = n_outer * n_inner // H
    rounds = (groups - 1).bit_length()
    me = lax.axis_index("outer") * n_inner + lax.axis_index("inner")
    group, place = me // H, me % H
    c, e = place // 2, place % 2

    def device(index):
        return (index // n_inner, index % n_inner)

    def remote(src, dst, send, recv, target):
        return pltpu.make_async_remote_copy(
            src_ref=src, dst_ref=dst, send_sem=send, recv_sem=recv,
            device_id=device(target), device_id_type=MESH,
        )

    partner = group * H + 2 * c + (1 - e)

    def mate(j):
        return group * H + 2 * j + e

    def cols(j, width):
        return pl.ds(pl.multiple_of(j * width, width), width)

    def load(which, hbm, vmem, j):
        return pltpu.make_async_copy(hbm.at[:, cols(j, PW)], vmem.at[:, cols(j, PW)], load_sem.at[which, j])

    barrier = pltpu.get_barrier_semaphore()

    def greet(target):
        pl.semaphore_signal(barrier, inc=1, device_id=device(target), device_id_type=MESH)

    greet(partner)
    for s in range(1, PAIRS):
        greet(mate((c + s) % PAIRS))
    expected = PAIRS
    for d in range(rounds):
        step = 1 << d
        up, down = group + step < groups, group >= step

        @pl.when(up)
        def _():
            greet(me + step * H)

        @pl.when(down)
        def _():
            greet(me - step * H)

        expected = expected + jnp.where(up, 1, 0) + jnp.where(down, 1, 0)

    for s in range(PAIRS):
        j = (c + ORDER[s]) % PAIRS
        load(0, k_hbm, k, j).start()
        load(1, v_hbm, v, j).start()
    for j in range(PAIRS):
        load(2, q_hbm, q, j).start()

    def pair_copy(j):
        return remote(local.at[2 * j + 1 - e], pair_buf.at[j], pair_send.at[j], pair_recv.at[j], partner)

    def up_copy(j, slot):
        return remote(chip.at[j], up_buf.at[slot], up_send.at[j], up_recv.at[slot], mate(j))

    def chip_sum(s):
        j = (c + ORDER[s]) % PAIRS
        pair_copy(j).wait_recv()
        total = local[2 * j + e] + pair_buf[j]
        if ORDER[s]:
            chip[j] = total
            up_copy(j, c).start()
        else:
            up_buf[c] = total

    for s in range(PAIRS):
        j = (c + ORDER[s]) % PAIRS
        load(0, k_hbm, k, j).wait()
        load(1, v_hbm, v, j).wait()
        both = lax.dot_general(
            k[:, cols(j, PW)], v[:, cols(j, PW)], (((0,), (0,)), ((), ())), preferred_element_type=F32
        )
        local[2 * j] = both[:DH, :DH]
        local[2 * j + 1] = both[DH:, DH:]
        if s == 0:
            pl.semaphore_wait(barrier, expected)
        pair_copy(j).start()
        if s > 0:
            chip_sum(s - 1)
    chip_sum(PAIRS - 1)

    for j in range(PAIRS):
        load(2, q_hbm, q, j).wait()

    causal = lax.broadcasted_iota(jnp.int32, (CHUNK, CHUNK), 0) >= lax.broadcasted_iota(
        jnp.int32, (CHUNK, CHUNK), 1
    )

    def store(h):
        return pltpu.make_async_copy(pre.at[:, cols(h, DH)], pre_hbm.at[:, cols(h, DH)], store_sem.at[h])

    def head(h, _):
        running = None
        for b in range(tok // CHUNK):
            at = (pl.ds(b * CHUNK, CHUNK), cols(h, DH))
            qc, kc, vc = q[at], k[at], v[at]
            scores = lax.dot_general(qc, kc, (((1,), (1,)), ((), ())), preferred_element_type=F32)
            weights = jnp.where(causal, scores, 0.0).astype(BF16)
            part = jnp.dot(weights, vc, preferred_element_type=F32)
            if b > 0:
                part = part + jnp.dot(qc, running.astype(BF16), preferred_element_type=F32)
            pre[at] = part
            if b + 1 < tok // CHUNK:
                state = lax.dot_general(kc, vc, (((0,), (0,)), ((), ())), preferred_element_type=F32)
                running = state if running is None else running + state
        store(h).start()
        return 0

    lax.fori_loop(0, 3, head, 0)

    for s in range(1, PAIRS):
        j = (c + s) % PAIRS
        up_copy(j, j).wait_recv()
    zs[0] = up_buf[0] + up_buf[1] + up_buf[2] + up_buf[3]
    zx[...] = jnp.zeros_like(zx)

    def z_copy(d, target):
        return remote(zs.at[d], zb.at[d], z_send.at[d], z_recv.at[d], target)

    splits = [3 + (3 * (d + 1)) // rounds if rounds else 6 for d in range(rounds)]
    begin = 3
    for d in range(rounds):
        step = 1 << d

        @pl.when(group + step < groups)
        def _():
            z_copy(d, me + step * H).start()

        lax.fori_loop(begin, splits[d], head, 0)
        begin = splits[d]

        @pl.when(group >= step)
        def _():
            z_copy(d, me - step * H).wait_recv()
            zx[...] = zx[...] + zb[d]

        if d + 1 < rounds:
            @pl.when(group >= step)
            def _():
                zs[d + 1] = zs[d] + zb[d]

            @pl.when(group < step)
            def _():
                zs[d + 1] = zs[d]

    running = zx[...]
    for i in range(PAIRS):
        down_src[i] = running
        if i + 1 < PAIRS:
            running = running + up_buf[i]

    def down_copy(j, slot):
        return remote(down_src.at[j], down_buf.at[slot], down_send.at[j], down_recv.at[slot], mate(j))

    for s in range(1, PAIRS):
        down_copy((c + s) % PAIRS, c).start()
    down_buf[c] = down_src[c]

    def fwd_copy(j):
        return remote(fwd.at[j], pd.at[j], fwd_send.at[j], fwd_recv.at[j], partner)

    def spread(s):
        j = (c + s) % PAIRS
        if s:
            down_copy(j, j).wait_recv()
        first = down_buf[j]
        fwd[j] = jnp.where(e == 0, first + local[2 * j], first)
        fwd_copy(j).start()
        s_ref[2 * j + e] = jnp.where(e == 1, first + pair_buf[j], first).astype(BF16)

    spread(0)
    lax.fori_loop(begin, H, head, 0)
    for s in range(1, PAIRS):
        spread(s)
    for s in range(PAIRS):
        j = (c + s) % PAIRS
        fwd_copy(j).wait_recv()
        s_ref[2 * j + 1 - e] = pd[j].astype(BF16)

    for s in range(PAIRS):
        j = (c + s) % PAIRS
        pair_copy(j).wait_send()
        fwd_copy(j).wait_send()
        if s:
            up_copy(j, c).wait_send()
            down_copy(j, c).wait_send()
    for d in range(rounds):
        @pl.when(group + (1 << d) < groups)
        def _():
            z_copy(d, me + (1 << d) * H).wait_send()
    for h in range(H):
        store(h).wait()


def scan_states(n_outer, n_inner, queries, keys, values):
    tok, width = queries.shape
    rounds = max(1, (n_outer * n_inner // H - 1).bit_length())
    state = lambda count: pltpu.VMEM((count, DH, DH), F32)
    sems = lambda *shape: pltpu.SemaphoreType.DMA(shape)
    whole = pltpu.VMEM((tok, width), BF16)
    return pl.pallas_call(
        functools.partial(scan_kernel, n_outer, n_inner),
        out_shape=(
            jax.ShapeDtypeStruct((H, DH, DH), BF16),
            jax.ShapeDtypeStruct((tok, width), F32),
        ),
        in_specs=[pl.BlockSpec(memory_space=pl.ANY)] * 3,
        out_specs=(pl.BlockSpec(memory_space=pltpu.VMEM), pl.BlockSpec(memory_space=pl.ANY)),
        scratch_shapes=[
            whole, whole, whole, pltpu.VMEM((tok, width), F32),
            state(H), state(PAIRS), state(PAIRS), state(PAIRS),
            state(rounds), state(rounds), pltpu.VMEM((DH, DH), F32),
            state(PAIRS), state(PAIRS), state(PAIRS), state(PAIRS),
            sems(3, PAIRS), sems(H), sems(PAIRS), sems(PAIRS), sems(PAIRS), sems(PAIRS),
            sems(rounds), sems(rounds), sems(PAIRS), sems(PAIRS), sems(PAIRS), sems(PAIRS),
        ],
        compiler_params=pltpu.CompilerParams(
            collective_id=0, has_side_effects=True, vmem_limit_bytes=40 * 1024 * 1024
        ),
        name="scan_states",
    )(queries, keys, values)


def finish_kernel(pre, q, s, gain, w_hbm, out, w, diag, normed, w_sem):
    def load(j):
        rows = pl.ds(j * PW, PW)
        return pltpu.make_async_copy(w_hbm.at[rows, :], w.at[rows, :], w_sem.at[j])

    first = pl.program_id(0) == 0

    @pl.when(first)
    def _():
        for j in range(PAIRS):
            load(j).start()
        diag[...] = jnp.zeros_like(diag)
        for h in range(H):
            at = pl.ds((h % 2) * DH, DH)
            diag[h // 2, at, at] = s[h]

    for j in range(PAIRS):
        at = slice(j * PW, (j + 1) * PW)
        both = pre[:, at] + jnp.dot(q[:, at], diag[j], preferred_element_type=F32)
        for half in range(2):
            attended = both[:, half * DH:(half + 1) * DH]
            at_head = slice(j * PW + half * DH, j * PW + (half + 1) * DH)
            mean_square = jnp.mean(attended * attended, axis=-1, keepdims=True)
            scaled = attended * lax.rsqrt(mean_square + 1e-06) * gain[:, at_head]
            normed[:, at_head] = scaled.astype(BF16)

    @pl.when(first)
    def _():
        for j in range(PAIRS):
            load(j).wait()

    tile = 512
    for n in range(out.shape[1] // tile):
        at = slice(n * tile, (n + 1) * tile)
        out[:, at] = jnp.dot(normed[...], w[:, at], preferred_element_type=F32).astype(BF16)


def finish(pre, queries, states, norm_gain, out_weight):
    tok, width = queries.shape
    model = out_weight.shape[1]
    return pl.pallas_call(
        finish_kernel,
        out_shape=jax.ShapeDtypeStruct((tok, model), BF16),
        grid=(tok // ROWS,),
        in_specs=[
            pl.BlockSpec((ROWS, width), lambda i: (i, 0)),
            pl.BlockSpec((ROWS, width), lambda i: (i, 0)),
            pl.BlockSpec((H, DH, DH), lambda i: (0, 0, 0)),
            pl.BlockSpec((1, width), lambda i: (0, 0)),
            pl.BlockSpec(memory_space=pl.ANY),
        ],
        out_specs=pl.BlockSpec((ROWS, model), lambda i: (i, 0)),
        scratch_shapes=[
            pltpu.VMEM((width, model), BF16),
            pltpu.VMEM((PAIRS, PW, PW), BF16),
            pltpu.VMEM((ROWS, width), BF16),
            pltpu.SemaphoreType.DMA((PAIRS,)),
        ],
        compiler_params=pltpu.CompilerParams(vmem_limit_bytes=40 * 1024 * 1024),
        name="norm_and_project",
    )(pre, queries, states, norm_gain.reshape(1, width), out_weight)


def solution(mesh):
    n_outer, n_inner = mesh.shape["outer"], mesh.shape["inner"]

    def on_device(queries, keys, values, norm_gain, out_weight):
        states, pre = scan_states(n_outer, n_inner, queries, keys, values)
        return finish(pre, queries, states, norm_gain, out_weight)

    rows = P(("outer", "inner"), None)
    return jax.shard_map(
        on_device,
        mesh=mesh,
        in_specs=(rows, rows, rows, P(), P()),
        out_specs=rows,
        check_vma=False,
    )
```

```python
import functools

import jax
import jax.numpy as jnp
from jax import lax
from jax.experimental import pallas as pl
from jax.experimental.pallas import tpu as pltpu
from jax.sharding import PartitionSpec as P

H = 8
DH = 128
PAIRS = H // 2
PW = 2 * DH
CHUNK = 256
ROWS = 256
TILE = 512
FINISH_MIB = 20
F32 = jnp.float32
BF16 = jnp.bfloat16
MESH = pl.DeviceIdType.MESH
ORDER = (1, 3, 2, 0)


def scan_kernel(
    n_outer, n_inner, q_hbm, k_hbm, v_hbm, s_ref, pre,
    q, k, v, local, pair_buf, chip, up_buf, zs, zb, zx, down_src, down_buf, fwd, pd,
    load_sem, pair_send, pair_recv, up_send, up_recv, z_send, z_recv,
    down_send, down_recv, fwd_send, fwd_recv,
):
    tok = q.shape[0]
    groups = n_outer * n_inner // H
    rounds = (groups - 1).bit_length()
    me = lax.axis_index("outer") * n_inner + lax.axis_index("inner")
    group, place = me // H, me % H
    c, e = place // 2, place % 2

    def device(index):
        return (index // n_inner, index % n_inner)

    def remote(src, dst, send, recv, target):
        return pltpu.make_async_remote_copy(
            src_ref=src, dst_ref=dst, send_sem=send, recv_sem=recv,
            device_id=device(target), device_id_type=MESH,
        )

    partner = group * H + 2 * c + (1 - e)

    def mate(j):
        return group * H + 2 * j + e

    def cols(j, width):
        return pl.ds(pl.multiple_of(j * width, width), width)

    def load(which, hbm, vmem, j):
        return pltpu.make_async_copy(hbm.at[:, cols(j, PW)], vmem.at[:, cols(j, PW)], load_sem.at[which, j])

    barrier = pltpu.get_barrier_semaphore()

    def greet(target):
        pl.semaphore_signal(barrier, inc=1, device_id=device(target), device_id_type=MESH)

    greet(partner)
    for s in range(1, PAIRS):
        greet(mate((c + s) % PAIRS))
    expected = PAIRS
    for d in range(rounds):
        step = 1 << d
        up, down = group + step < groups, group >= step

        @pl.when(up)
        def _():
            greet(me + step * H)

        @pl.when(down)
        def _():
            greet(me - step * H)

        expected = expected + jnp.where(up, 1, 0) + jnp.where(down, 1, 0)

    for s in range(PAIRS):
        j = (c + ORDER[s]) % PAIRS
        load(0, k_hbm, k, j).start()
        load(1, v_hbm, v, j).start()
    for j in range(PAIRS):
        load(2, q_hbm, q, j).start()

    def pair_copy(j):
        return remote(local.at[2 * j + 1 - e], pair_buf.at[j], pair_send.at[j], pair_recv.at[j], partner)

    def up_copy(j, slot):
        return remote(chip.at[j], up_buf.at[slot], up_send.at[j], up_recv.at[slot], mate(j))

    def chip_sum(s):
        j = (c + ORDER[s]) % PAIRS
        pair_copy(j).wait_recv()
        total = local[2 * j + e] + pair_buf[j]
        if ORDER[s]:
            chip[j] = total
            up_copy(j, c).start()
        else:
            up_buf[c] = total

    for s in range(PAIRS):
        j = (c + ORDER[s]) % PAIRS
        load(0, k_hbm, k, j).wait()
        load(1, v_hbm, v, j).wait()
        both = lax.dot_general(
            k[:, cols(j, PW)], v[:, cols(j, PW)], (((0,), (0,)), ((), ())), preferred_element_type=F32
        )
        local[2 * j] = both[:DH, :DH]
        local[2 * j + 1] = both[DH:, DH:]
        if s == 0:
            pl.semaphore_wait(barrier, expected)
        pair_copy(j).start()
        if s > 0:
            chip_sum(s - 1)
    chip_sum(PAIRS - 1)

    for j in range(PAIRS):
        load(2, q_hbm, q, j).wait()

    causal = lax.broadcasted_iota(jnp.int32, (CHUNK, CHUNK), 0) >= lax.broadcasted_iota(
        jnp.int32, (CHUNK, CHUNK), 1
    )

    def head(h, _):
        running = None
        for b in range(tok // CHUNK):
            at = (pl.ds(b * CHUNK, CHUNK), cols(h, DH))
            qc, kc, vc = q[at], k[at], v[at]
            scores = lax.dot_general(qc, kc, (((1,), (1,)), ((), ())), preferred_element_type=F32)
            weights = jnp.where(causal, scores, 0.0).astype(BF16)
            part = jnp.dot(weights, vc, preferred_element_type=F32)
            if b > 0:
                part = part + jnp.dot(qc, running.astype(BF16), preferred_element_type=F32)
            pre[at] = part
            if b + 1 < tok // CHUNK:
                state = lax.dot_general(kc, vc, (((0,), (0,)), ((), ())), preferred_element_type=F32)
                running = state if running is None else running + state
        return 0

    lax.fori_loop(0, 3, head, 0)

    for s in range(1, PAIRS):
        j = (c + s) % PAIRS
        up_copy(j, j).wait_recv()
    zs[0] = up_buf[0] + up_buf[1] + up_buf[2] + up_buf[3]
    zx[...] = jnp.zeros_like(zx)

    def z_copy(d, target):
        return remote(zs.at[d], zb.at[d], z_send.at[d], z_recv.at[d], target)

    splits = [3 + (3 * (d + 1)) // rounds if rounds else 6 for d in range(rounds)]
    begin = 3
    for d in range(rounds):
        step = 1 << d

        @pl.when(group + step < groups)
        def _():
            z_copy(d, me + step * H).start()

        lax.fori_loop(begin, splits[d], head, 0)
        begin = splits[d]

        @pl.when(group >= step)
        def _():
            z_copy(d, me - step * H).wait_recv()
            zx[...] = zx[...] + zb[d]

        if d + 1 < rounds:
            @pl.when(group >= step)
            def _():
                zs[d + 1] = zs[d] + zb[d]

            @pl.when(group < step)
            def _():
                zs[d + 1] = zs[d]

    running = zx[...]
    for i in range(PAIRS):
        down_src[i] = running
        if i + 1 < PAIRS:
            running = running + up_buf[i]

    def down_copy(j, slot):
        return remote(down_src.at[j], down_buf.at[slot], down_send.at[j], down_recv.at[slot], mate(j))

    for s in range(1, PAIRS):
        down_copy((c + s) % PAIRS, c).start()
    down_buf[c] = down_src[c]

    def fwd_copy(j):
        return remote(fwd.at[j], pd.at[j], fwd_send.at[j], fwd_recv.at[j], partner)

    def spread(s):
        j = (c + s) % PAIRS
        if s:
            down_copy(j, j).wait_recv()
        first = down_buf[j]
        fwd[j] = jnp.where(e == 0, first + local[2 * j], first)
        fwd_copy(j).start()
        s_ref[2 * j + e] = jnp.where(e == 1, first + pair_buf[j], first).astype(BF16)

    spread(0)
    lax.fori_loop(begin, H, head, 0)
    for s in range(1, PAIRS):
        spread(s)
    for s in range(PAIRS):
        j = (c + s) % PAIRS
        fwd_copy(j).wait_recv()
        s_ref[2 * j + 1 - e] = pd[j].astype(BF16)

    for s in range(PAIRS):
        j = (c + s) % PAIRS
        pair_copy(j).wait_send()
        fwd_copy(j).wait_send()
        if s:
            up_copy(j, c).wait_send()
            down_copy(j, c).wait_send()
    for d in range(rounds):
        @pl.when(group + (1 << d) < groups)
        def _():
            z_copy(d, me + (1 << d) * H).wait_send()


def scan_states(n_outer, n_inner, queries, keys, values):
    tok, width = queries.shape
    rounds = max(1, (n_outer * n_inner // H - 1).bit_length())
    state = lambda count: pltpu.VMEM((count, DH, DH), F32)
    sems = lambda *shape: pltpu.SemaphoreType.DMA(shape)
    whole = pltpu.VMEM((tok, width), BF16)
    return pl.pallas_call(
        functools.partial(scan_kernel, n_outer, n_inner),
        out_shape=(
            jax.ShapeDtypeStruct((H, DH, DH), BF16),
            jax.ShapeDtypeStruct((tok, width), F32),
        ),
        in_specs=[pl.BlockSpec(memory_space=pl.ANY)] * 3,
        out_specs=(pl.BlockSpec(memory_space=pltpu.VMEM),) * 2,
        scratch_shapes=[
            whole, whole, whole,
            state(H), state(PAIRS), state(PAIRS), state(PAIRS),
            state(rounds), state(rounds), pltpu.VMEM((DH, DH), F32),
            state(PAIRS), state(PAIRS), state(PAIRS), state(PAIRS),
            sems(3, PAIRS), sems(PAIRS), sems(PAIRS), sems(PAIRS), sems(PAIRS),
            sems(rounds), sems(rounds), sems(PAIRS), sems(PAIRS), sems(PAIRS), sems(PAIRS),
        ],
        compiler_params=pltpu.CompilerParams(
            collective_id=0, has_side_effects=True, vmem_limit_bytes=32 * 1024 * 1024
        ),
        name="scan_states",
    )(queries, keys, values)


def finish_kernel(pre, q, s, gain, w, out_hbm, diag, normed, out, out_sem):
    tok, model = out.shape
    diag[...] = jnp.zeros_like(diag)
    for h in range(H):
        at = pl.ds((h % 2) * DH, DH)
        diag[h // 2, at, at] = s[h]

    def norm(r):
        rows = slice(r * ROWS, (r + 1) * ROWS)
        for j in range(PAIRS):
            at = slice(j * PW, (j + 1) * PW)
            both = pre[rows, at] + jnp.dot(q[rows, at], diag[j], preferred_element_type=F32)
            for half in range(2):
                attended = both[:, half * DH:(half + 1) * DH]
                at_head = slice(j * PW + half * DH, j * PW + (half + 1) * DH)
                mean_square = jnp.mean(attended * attended, axis=-1, keepdims=True)
                scaled = attended * lax.rsqrt(mean_square + 1e-06) * gain[:, at_head]
                normed[r % 2, :, at_head] = scaled.astype(BF16)

    def store(r):
        rows = pl.ds(r * ROWS, ROWS)
        return pltpu.make_async_copy(out.at[rows, :], out_hbm.at[rows, :], out_sem.at[r])

    chunks = tok // ROWS
    norm(0)
    for r in range(chunks):
        if r + 1 < chunks:
            norm(r + 1)
        rows = slice(r * ROWS, (r + 1) * ROWS)
        for n in range(model // TILE):
            at = slice(n * TILE, (n + 1) * TILE)
            out[rows, at] = jnp.dot(normed[r % 2], w[:, at], preferred_element_type=F32).astype(BF16)
        store(r).start()
    for r in range(chunks):
        store(r).wait()


def finish(pre, queries, states, norm_gain, out_weight):
    tok, width = queries.shape
    model = out_weight.shape[1]
    return pl.pallas_call(
        finish_kernel,
        out_shape=jax.ShapeDtypeStruct((tok, model), BF16),
        in_specs=[pl.BlockSpec(memory_space=pltpu.VMEM)] * 5,
        out_specs=pl.BlockSpec(memory_space=pl.ANY),
        scratch_shapes=[
            pltpu.VMEM((PAIRS, PW, PW), BF16),
            pltpu.VMEM((2, ROWS, width), BF16),
            pltpu.VMEM((tok, model), BF16),
            pltpu.SemaphoreType.DMA((tok // ROWS,)),
        ],
        compiler_params=pltpu.CompilerParams(vmem_limit_bytes=FINISH_MIB * 1024 * 1024),
        name="norm_and_project",
    )(pre, queries, states, norm_gain.reshape(1, width), out_weight)


def solution(mesh):
    n_outer, n_inner = mesh.shape["outer"], mesh.shape["inner"]

    def on_device(queries, keys, values, norm_gain, out_weight):
        held = [pltpu.with_memory_space_constraint(x, pltpu.HBM) for x in (queries, keys, values)]
        states, pre = scan_states(n_outer, n_inner, *held)
        return finish(pre, queries, states, norm_gain, out_weight)

    rows = P(("outer", "inner"), None)
    return jax.shard_map(
        on_device,
        mesh=mesh,
        in_specs=(rows, rows, rows, P(), P()),
        out_specs=rows,
        check_vma=False,
    )
```

```python
import functools

import jax
import jax.numpy as jnp
from jax import lax
from jax.experimental import pallas as pl
from jax.experimental.pallas import tpu as pltpu
from jax.sharding import PartitionSpec as P

H = 8
DH = 128
PAIRS = H // 2
PW = 2 * DH
CHUNK = 256
ROWS = 512
TILE = 512
F32 = jnp.float32
BF16 = jnp.bfloat16
MESH = pl.DeviceIdType.MESH
ORDER = (1, 3, 2, 0)


def scan_kernel(
    n_outer, n_inner, q_hbm, k_hbm, v_hbm, w_hbm, gain_hbm, normed, w,
    gain, q, k, v, pre, low, diag, local, pair_buf, chip, up_buf, zs, zb, zx, down_src, down_buf, fwd, pd,
    load_sem, w_sem, gain_sem, pair_send, pair_recv, up_send, up_recv, z_send, z_recv,
    down_send, down_recv, fwd_send, fwd_recv,
):
    tok = q.shape[0]
    blocks = tok // CHUNK
    groups = n_outer * n_inner // H
    rounds = (groups - 1).bit_length()
    me = lax.axis_index("outer") * n_inner + lax.axis_index("inner")
    group, place = me // H, me % H
    c, e = place // 2, place % 2

    def device(index):
        return (index // n_inner, index % n_inner)

    def remote(src, dst, send, recv, target):
        return pltpu.make_async_remote_copy(
            src_ref=src, dst_ref=dst, send_sem=send, recv_sem=recv,
            device_id=device(target), device_id_type=MESH,
        )

    partner = group * H + 2 * c + (1 - e)

    def mate(j):
        return group * H + 2 * j + e

    def cols(j, width):
        return pl.ds(pl.multiple_of(j * width, width), width)

    def load(which, hbm, vmem, j):
        return pltpu.make_async_copy(hbm.at[:, cols(j, PW)], vmem.at[:, cols(j, PW)], load_sem.at[which, j])

    barrier = pltpu.get_barrier_semaphore()

    def greet(target):
        pl.semaphore_signal(barrier, inc=1, device_id=device(target), device_id_type=MESH)

    greet(partner)
    for s in range(1, PAIRS):
        greet(mate((c + s) % PAIRS))
    expected = PAIRS
    for d in range(rounds):
        step = 1 << d
        up, down = group + step < groups, group >= step

        @pl.when(up)
        def _():
            greet(me + step * H)

        @pl.when(down)
        def _():
            greet(me - step * H)

        expected = expected + jnp.where(up, 1, 0) + jnp.where(down, 1, 0)

    for s in range(PAIRS):
        j = (c + ORDER[s]) % PAIRS
        load(0, k_hbm, k, j).start()
        load(1, v_hbm, v, j).start()
    for j in range(PAIRS):
        load(2, q_hbm, q, j).start()
    whole_w = pltpu.make_async_copy(w_hbm, w, w_sem)
    whole_w.start()
    whole_gain = pltpu.make_async_copy(gain_hbm, gain, gain_sem)
    whole_gain.start()
    diag[...] = jnp.zeros_like(diag)

    def pair_copy(j):
        return remote(local.at[2 * j + 1 - e], pair_buf.at[j], pair_send.at[j], pair_recv.at[j], partner)

    def up_copy(j, slot):
        return remote(chip.at[j], up_buf.at[slot], up_send.at[j], up_recv.at[slot], mate(j))

    def chip_sum(s):
        j = (c + ORDER[s]) % PAIRS
        pair_copy(j).wait_recv()
        total = local[2 * j + e] + pair_buf[j]
        if ORDER[s]:
            chip[j] = total
            up_copy(j, c).start()
        else:
            up_buf[c] = total

    for s in range(PAIRS):
        j = (c + ORDER[s]) % PAIRS
        load(0, k_hbm, k, j).wait()
        load(1, v_hbm, v, j).wait()
        sums = [None, None]
        for b in range(blocks):
            at = (pl.ds(b * CHUNK, CHUNK), cols(j, PW))
            both = lax.dot_general(k[at], v[at], (((0,), (0,)), ((), ())), preferred_element_type=F32)
            for half in range(2):
                own = both[half * DH:(half + 1) * DH, half * DH:(half + 1) * DH]
                sums[half] = own if b == 0 else sums[half] + own
                if b + 1 < blocks:
                    low[2 * j + half, b] = sums[half].astype(BF16)
        local[2 * j] = sums[0]
        local[2 * j + 1] = sums[1]
        if s == 0:
            pl.semaphore_wait(barrier, expected)
        pair_copy(j).start()
        if s > 0:
            chip_sum(s - 1)
    chip_sum(PAIRS - 1)

    for j in range(PAIRS):
        load(2, q_hbm, q, j).wait()

    causal = lax.broadcasted_iota(jnp.int32, (CHUNK, CHUNK), 0) >= lax.broadcasted_iota(
        jnp.int32, (CHUNK, CHUNK), 1
    )

    def causal_part(j, _):
        weights = {}
        for half in range(2):
            for b in range(blocks):
                at = (pl.ds(b * CHUNK, CHUNK), cols(2 * j + half, DH))
                scores = lax.dot_general(q[at], k[at], (((1,), (1,)), ((), ())), preferred_element_type=F32)
                weights[half, b] = jnp.where(causal, scores, 0.0).astype(BF16)
        for half in range(2):
            for b in range(blocks):
                at = (pl.ds(b * CHUNK, CHUNK), cols(2 * j + half, DH))
                part = jnp.dot(weights[half, b], v[at], preferred_element_type=F32)
                if b > 0:
                    part = part + jnp.dot(q[at], low[2 * j + half, b - 1], preferred_element_type=F32)
                pre[at] = part
        return 0

    lax.fori_loop(0, 2, causal_part, 0)

    for s in range(1, PAIRS):
        j = (c + s) % PAIRS
        up_copy(j, j).wait_recv()
    zs[0] = up_buf[0] + up_buf[1] + up_buf[2] + up_buf[3]
    zx[...] = jnp.zeros_like(zx)

    def z_copy(d, target):
        return remote(zs.at[d], zb.at[d], z_send.at[d], z_recv.at[d], target)

    splits = [2 + (2 * (d + 1)) // rounds for d in range(rounds)]
    begin = 2
    for d in range(rounds):
        step = 1 << d

        @pl.when(group + step < groups)
        def _():
            z_copy(d, me + step * H).start()

        lax.fori_loop(begin, splits[d], causal_part, 0)
        begin = splits[d]

        @pl.when(group >= step)
        def _():
            z_copy(d, me - step * H).wait_recv()
            zx[...] = zx[...] + zb[d]

        if d + 1 < rounds:
            @pl.when(group >= step)
            def _():
                zs[d + 1] = zs[d] + zb[d]

            @pl.when(group < step)
            def _():
                zs[d + 1] = zs[d]

    running = zx[...]
    for i in range(PAIRS):
        down_src[i] = running
        if i + 1 < PAIRS:
            running = running + up_buf[i]

    def down_copy(j, slot):
        return remote(down_src.at[j], down_buf.at[slot], down_send.at[j], down_recv.at[slot], mate(j))

    for s in range(1, PAIRS):
        down_copy((c + s) % PAIRS, c).start()
    down_buf[c] = down_src[c]

    def fwd_copy(j):
        return remote(fwd.at[j], pd.at[j], fwd_send.at[j], fwd_recv.at[j], partner)

    def spread(s):
        j = (c + s) % PAIRS
        if s:
            down_copy(j, j).wait_recv()
        first = down_buf[j]
        fwd[j] = jnp.where(e == 0, first + local[2 * j], first)
        fwd_copy(j).start()
        half = pl.ds(pl.multiple_of(e * DH, DH), DH)
        diag[s, half, half] = jnp.where(e == 1, first + pair_buf[j], first).astype(BF16)

    def norm(s):
        j = (c + s) % PAIRS
        fwd_copy(j).wait_recv()
        half = pl.ds(pl.multiple_of((1 - e) * DH, DH), DH)
        diag[s, half, half] = pd[j].astype(BF16)
        carried = diag[s]
        for b in range(blocks):
            rows = pl.ds(b * CHUNK, CHUNK)
            both = pre[rows, cols(j, PW)] + jnp.dot(q[rows, cols(j, PW)], carried, preferred_element_type=F32)
            for i in range(2):
                attended = both[:, i * DH:(i + 1) * DH]
                mean_square = jnp.mean(attended * attended, axis=-1, keepdims=True)
                scaled = attended * lax.rsqrt(mean_square + 1e-06) * gain[:, cols(2 * j + i, DH)]
                normed[rows, cols(2 * j + i, DH)] = scaled.astype(BF16)

    whole_gain.wait()
    spread(0)
    lax.fori_loop(begin, PAIRS, causal_part, 0)
    for s in range(1, PAIRS):
        spread(s)
        norm(s - 1)
    norm(PAIRS - 1)
    whole_w.wait()

    for s in range(PAIRS):
        j = (c + s) % PAIRS
        pair_copy(j).wait_send()
        fwd_copy(j).wait_send()
        if s:
            up_copy(j, c).wait_send()
            down_copy(j, c).wait_send()
    for d in range(rounds):
        @pl.when(group + (1 << d) < groups)
        def _():
            z_copy(d, me + (1 << d) * H).wait_send()


def scan_and_norm(n_outer, n_inner, queries, keys, values, norm_gain, out_weight):
    tok, width = queries.shape
    rounds = max(1, (n_outer * n_inner // H - 1).bit_length())
    state = lambda count: pltpu.VMEM((count, DH, DH), F32)
    sems = lambda *shape: pltpu.SemaphoreType.DMA(shape)
    whole = pltpu.VMEM((tok, width), BF16)
    vmem = pl.BlockSpec(memory_space=pltpu.VMEM)
    held = [pltpu.with_memory_space_constraint(x, pltpu.HBM) for x in (queries, keys, values, out_weight, norm_gain.reshape(1, width))]
    return pl.pallas_call(
        functools.partial(scan_kernel, n_outer, n_inner),
        out_shape=(
            jax.ShapeDtypeStruct((tok, width), BF16),
            jax.ShapeDtypeStruct(out_weight.shape, BF16),
        ),
        in_specs=[pl.BlockSpec(memory_space=pl.ANY)] * 5,
        out_specs=(vmem, vmem),
        scratch_shapes=[
            pltpu.VMEM((1, width), F32), whole, whole, whole, pltpu.VMEM((tok, width), F32),
            pltpu.VMEM((H, max(1, tok // CHUNK - 1), DH, DH), BF16), pltpu.VMEM((PAIRS, PW, PW), BF16),
            state(H), state(PAIRS), state(PAIRS), state(PAIRS),
            state(rounds), state(rounds), pltpu.VMEM((DH, DH), F32),
            state(PAIRS), state(PAIRS), state(PAIRS), state(PAIRS),
            sems(3, PAIRS), pltpu.SemaphoreType.DMA, pltpu.SemaphoreType.DMA, sems(PAIRS), sems(PAIRS), sems(PAIRS), sems(PAIRS),
            sems(rounds), sems(rounds), sems(PAIRS), sems(PAIRS), sems(PAIRS), sems(PAIRS),
        ],
        compiler_params=pltpu.CompilerParams(
            collective_id=0, has_side_effects=True, vmem_limit_bytes=32 * 1024 * 1024
        ),
        name="scan_and_norm",
    )(*held)


def project_kernel(normed, w, out_hbm, out, out_sem):
    tok, model = out.shape
    copies = []
    for r in range(tok // ROWS):
        for n in range(model // TILE):
            rows, at = pl.ds(r * ROWS, ROWS), pl.ds(n * TILE, TILE)
            out[rows, at] = jnp.dot(normed[rows, :], w[:, at], preferred_element_type=F32).astype(BF16)
            copy = pltpu.make_async_copy(out.at[rows, at], out_hbm.at[rows, at], out_sem.at[r, n])
            copy.start()
            copies.append(copy)
    for copy in copies:
        copy.wait()


def project(normed, out_weight):
    tok, model = normed.shape[0], out_weight.shape[1]
    return pl.pallas_call(
        project_kernel,
        out_shape=jax.ShapeDtypeStruct((tok, model), BF16),
        in_specs=[pl.BlockSpec(memory_space=pltpu.VMEM)] * 2,
        out_specs=pl.BlockSpec(memory_space=pl.ANY),
        scratch_shapes=[
            pltpu.VMEM((tok, model), BF16),
            pltpu.SemaphoreType.DMA((tok // ROWS, model // TILE)),
        ],
        compiler_params=pltpu.CompilerParams(vmem_limit_bytes=20 * 1024 * 1024),
        name="project",
    )(normed, out_weight)


def solution(mesh):
    n_outer, n_inner = mesh.shape["outer"], mesh.shape["inner"]

    def on_device(queries, keys, values, norm_gain, out_weight):
        normed, weight = scan_and_norm(n_outer, n_inner, queries, keys, values, norm_gain, out_weight)
        return project(normed, weight)

    rows = P(("outer", "inner"), None)
    return jax.shard_map(
        on_device,
        mesh=mesh,
        in_specs=(rows, rows, rows, P(), P()),
        out_specs=rows,
        check_vma=False,
    )
```

```python
import functools

import jax
import jax.numpy as jnp
from jax import lax
from jax.experimental import pallas as pl
from jax.experimental.pallas import tpu as pltpu
from jax.sharding import PartitionSpec as P

H = 8
DH = 128
PAIRS = H // 2
PW = 2 * DH
CHUNK = 256
ROWS = 512
TILE = 512
F32 = jnp.float32
BF16 = jnp.bfloat16
MESH = pl.DeviceIdType.MESH
ORDER = (1, 3, 2, 0)
PART = DH // 2
PARTS = (slice(0, PART), slice(PART, DH))


def scan_kernel(
    n_outer, n_inner, q_hbm, k_hbm, v_hbm, w_hbm, gain_hbm, normed, w,
    gain, q, k, v, pre, low, diag, local, pair_buf, chip, up_buf, zs, zb, zx, down_src, down_buf, fwd, pd,
    load_sem, w_sem, gain_sem, pair_send, pair_recv, up_send, up_recv, z_send, z_recv,
    down_send, down_recv, fwd_send, fwd_recv,
):
    tok = q.shape[0]
    blocks = tok // CHUNK
    groups = n_outer * n_inner // H
    rounds = (groups - 1).bit_length()
    me = lax.axis_index("outer") * n_inner + lax.axis_index("inner")
    group, place = me // H, me % H
    c, e = place // 2, place % 2

    def device(index):
        return (index // n_inner, index % n_inner)

    def remote(src, dst, send, recv, target):
        return pltpu.make_async_remote_copy(
            src_ref=src, dst_ref=dst, send_sem=send, recv_sem=recv,
            device_id=device(target), device_id_type=MESH,
        )

    partner = group * H + 2 * c + (1 - e)

    def mate(j):
        return group * H + 2 * j + e

    def cols(j, width):
        return pl.ds(pl.multiple_of(j * width, width), width)

    def load(which, hbm, vmem, j):
        return pltpu.make_async_copy(hbm.at[:, cols(j, PW)], vmem.at[:, cols(j, PW)], load_sem.at[which, j])

    barrier = pltpu.get_barrier_semaphore()

    def greet(target):
        pl.semaphore_signal(barrier, inc=1, device_id=device(target), device_id_type=MESH)

    greet(partner)
    for s in range(1, PAIRS):
        greet(mate((c + s) % PAIRS))
    expected = PAIRS
    for d in range(rounds):
        step = 1 << d
        up, down = group + step < groups, group >= step

        @pl.when(up)
        def _():
            greet(me + step * H)

        @pl.when(down)
        def _():
            greet(me - step * H)

        expected = expected + jnp.where(up, 1, 0) + jnp.where(down, 1, 0)

    for s in range(PAIRS):
        j = (c + ORDER[s]) % PAIRS
        load(0, k_hbm, k, j).start()
        load(1, v_hbm, v, j).start()
    for j in range(PAIRS):
        load(2, q_hbm, q, j).start()
    whole_w = pltpu.make_async_copy(w_hbm, w, w_sem)
    whole_w.start()
    whole_gain = pltpu.make_async_copy(gain_hbm, gain, gain_sem)
    whole_gain.start()
    diag[...] = jnp.zeros_like(diag)

    def pair_copy(j):
        return remote(local.at[2 * j + 1 - e], pair_buf.at[j], pair_send.at[j], pair_recv.at[j], partner)

    def part(p):
        return pl.ds(p * PART, PART)

    def up_copy(j, slot, p):
        return remote(
            chip.at[j, part(p)], up_buf.at[slot, part(p)], up_send.at[p, j], up_recv.at[p, slot], mate(j)
        )

    def chip_sum(s):
        j = (c + ORDER[s]) % PAIRS
        pair_copy(j).wait_recv()
        total = local[2 * j + e] + pair_buf[j]
        if ORDER[s]:
            chip[j] = total
            for p in range(2):
                up_copy(j, c, p).start()
        else:
            up_buf[c] = total

    for s in range(PAIRS):
        j = (c + ORDER[s]) % PAIRS
        load(0, k_hbm, k, j).wait()
        load(1, v_hbm, v, j).wait()
        sums = [None, None]
        for b in range(blocks):
            at = (pl.ds(b * CHUNK, CHUNK), cols(j, PW))
            both = lax.dot_general(k[at], v[at], (((0,), (0,)), ((), ())), preferred_element_type=F32)
            for half in range(2):
                own = both[half * DH:(half + 1) * DH, half * DH:(half + 1) * DH]
                sums[half] = own if b == 0 else sums[half] + own
                if b + 1 < blocks:
                    low[2 * j + half, b] = sums[half].astype(BF16)
        local[2 * j] = sums[0]
        local[2 * j + 1] = sums[1]
        if s == 0:
            pl.semaphore_wait(barrier, expected)
        pair_copy(j).start()
        if s > 0:
            chip_sum(s - 1)
    chip_sum(PAIRS - 1)

    for j in range(PAIRS):
        load(2, q_hbm, q, j).wait()

    causal = lax.broadcasted_iota(jnp.int32, (CHUNK, CHUNK), 0) >= lax.broadcasted_iota(
        jnp.int32, (CHUNK, CHUNK), 1
    )

    def causal_part(h, _):
        weights = []
        for b in range(blocks):
            at = (pl.ds(b * CHUNK, CHUNK), cols(h, DH))
            scores = lax.dot_general(q[at], k[at], (((1,), (1,)), ((), ())), preferred_element_type=F32)
            weights.append(jnp.where(causal, scores, 0.0).astype(BF16))
        for b in range(blocks):
            at = (pl.ds(b * CHUNK, CHUNK), cols(h, DH))
            inside = jnp.dot(weights[b], v[at], preferred_element_type=F32)
            if b > 0:
                inside = inside + jnp.dot(q[at], low[h, b - 1], preferred_element_type=F32)
            pre[at] = inside
        return 0

    done = 0

    def work(heads):
        nonlocal done
        until = min(H, done + heads)
        if until > done:
            lax.fori_loop(done, until, causal_part, 0)
        done = until

    def z_copy(d, target, p):
        return remote(zs.at[d, part(p)], zb.at[d, part(p)], z_send.at[p, d], z_recv.at[p, d], target)

    def z_start(d, p):
        @pl.when(group + (1 << d) < groups)
        def _():
            z_copy(d, me + (1 << d) * H, p).start()

    def z_take(d, p):
        rows = PARTS[p]

        @pl.when(group >= 1 << d)
        def _():
            z_copy(d, me - (1 << d) * H, p).wait_recv()
            zx[rows] = zx[rows] + zb[d, rows]

        if d + 1 < rounds:
            @pl.when(group >= 1 << d)
            def _():
                zs[d + 1, rows] = zs[d, rows] + zb[d, rows]

            @pl.when(group < 1 << d)
            def _():
                zs[d + 1, rows] = zs[d, rows]

    def down_copy(j, slot, p):
        return remote(
            down_src.at[j, part(p)], down_buf.at[slot, part(p)], down_send.at[p, j], down_recv.at[p, slot], mate(j)
        )

    def down_start(p):
        rows = PARTS[p]
        running = zx[rows]
        for i in range(PAIRS):
            down_src[i, rows] = running
            if i + 1 < PAIRS:
                running = running + up_buf[i, rows]
        for s in range(1, PAIRS):
            down_copy((c + s) % PAIRS, c, p).start()
        down_buf[c, rows] = down_src[c, rows]

    work(2)
    zx[...] = jnp.zeros_like(zx)
    for p in range(2):
        rows = PARTS[p]
        for s in range(1, PAIRS):
            j = (c + s) % PAIRS
            up_copy(j, j, p).wait_recv()
        zs[0, rows] = up_buf[0, rows] + up_buf[1, rows] + up_buf[2, rows] + up_buf[3, rows]
        z_start(0, p)
        work(1)
    for d in range(rounds):
        for p in range(2):
            z_take(d, p)
            if d + 1 < rounds:
                z_start(d + 1, p)
            else:
                down_start(p)
            work(1)
    work(H)

    def fwd_copy(j, p):
        return remote(fwd.at[j, part(p)], pd.at[j, part(p)], fwd_send.at[p, j], fwd_recv.at[p, j], partner)

    def spread(s, p):
        j = (c + s) % PAIRS
        rows = PARTS[p]
        if s:
            down_copy(j, j, p).wait_recv()
        first = down_buf[j, rows]
        fwd[j, rows] = jnp.where(e == 0, first + local[2 * j, rows], first)
        fwd_copy(j, p).start()
        at = pl.ds(pl.multiple_of(e * DH + p * PART, PART), PART)
        half = pl.ds(pl.multiple_of(e * DH, DH), DH)
        diag[s, at, half] = jnp.where(e == 1, first + pair_buf[j, rows], first).astype(BF16)

    def norm(s):
        j = (c + s) % PAIRS
        for p in range(2):
            fwd_copy(j, p).wait_recv()
        half = pl.ds(pl.multiple_of((1 - e) * DH, DH), DH)
        diag[s, half, half] = pd[j].astype(BF16)
        carried = diag[s]
        for b in range(blocks):
            rows = pl.ds(b * CHUNK, CHUNK)
            both = pre[rows, cols(j, PW)] + jnp.dot(q[rows, cols(j, PW)], carried, preferred_element_type=F32)
            for i in range(2):
                attended = both[:, i * DH:(i + 1) * DH]
                mean_square = jnp.mean(attended * attended, axis=-1, keepdims=True)
                scaled = attended * lax.rsqrt(mean_square + 1e-06) * gain[:, cols(2 * j + i, DH)]
                normed[rows, cols(2 * j + i, DH)] = scaled.astype(BF16)

    whole_gain.wait()
    for s in range(PAIRS):
        spread(s, 0)
    spread(0, 1)
    for s in range(1, PAIRS):
        spread(s, 1)
        norm(s - 1)
    norm(PAIRS - 1)
    whole_w.wait()

    for s in range(PAIRS):
        j = (c + s) % PAIRS
        pair_copy(j).wait_send()
        for p in range(2):
            fwd_copy(j, p).wait_send()
            if s:
                up_copy(j, c, p).wait_send()
                down_copy(j, c, p).wait_send()
    for d in range(rounds):
        @pl.when(group + (1 << d) < groups)
        def _():
            for p in range(2):
                z_copy(d, me + (1 << d) * H, p).wait_send()


def scan_and_norm(n_outer, n_inner, queries, keys, values, norm_gain, out_weight):
    tok, width = queries.shape
    rounds = max(1, (n_outer * n_inner // H - 1).bit_length())
    state = lambda count: pltpu.VMEM((count, DH, DH), F32)
    sems = lambda *shape: pltpu.SemaphoreType.DMA(shape)
    whole = pltpu.VMEM((tok, width), BF16)
    vmem = pl.BlockSpec(memory_space=pltpu.VMEM)
    held = [pltpu.with_memory_space_constraint(x, pltpu.HBM) for x in (queries, keys, values, out_weight, norm_gain.reshape(1, width))]
    return pl.pallas_call(
        functools.partial(scan_kernel, n_outer, n_inner),
        out_shape=(
            jax.ShapeDtypeStruct((tok, width), BF16),
            jax.ShapeDtypeStruct(out_weight.shape, BF16),
        ),
        in_specs=[pl.BlockSpec(memory_space=pl.ANY)] * 5,
        out_specs=(vmem, vmem),
        scratch_shapes=[
            pltpu.VMEM((1, width), F32), whole, whole, whole, pltpu.VMEM((tok, width), F32),
            pltpu.VMEM((H, max(1, tok // CHUNK - 1), DH, DH), BF16), pltpu.VMEM((PAIRS, PW, PW), BF16),
            state(H), state(PAIRS), state(PAIRS), state(PAIRS),
            state(rounds), state(rounds), pltpu.VMEM((DH, DH), F32),
            state(PAIRS), state(PAIRS), state(PAIRS), state(PAIRS),
            sems(3, PAIRS), pltpu.SemaphoreType.DMA, pltpu.SemaphoreType.DMA, sems(PAIRS), sems(PAIRS), sems(2, PAIRS), sems(2, PAIRS),
            sems(2, rounds), sems(2, rounds), sems(2, PAIRS), sems(2, PAIRS), sems(2, PAIRS), sems(2, PAIRS),
        ],
        compiler_params=pltpu.CompilerParams(
            collective_id=0, has_side_effects=True, vmem_limit_bytes=32 * 1024 * 1024
        ),
        name="scan_and_norm",
    )(*held)


def project_kernel(normed, w, out_hbm, out, out_sem):
    tok, model = out.shape
    copies = []
    for r in range(tok // ROWS):
        for n in range(model // TILE):
            rows, at = pl.ds(r * ROWS, ROWS), pl.ds(n * TILE, TILE)
            out[rows, at] = jnp.dot(normed[rows, :], w[:, at], preferred_element_type=F32).astype(BF16)
            copy = pltpu.make_async_copy(out.at[rows, at], out_hbm.at[rows, at], out_sem.at[r, n])
            copy.start()
            copies.append(copy)
    for copy in copies:
        copy.wait()


def project(normed, out_weight):
    tok, model = normed.shape[0], out_weight.shape[1]
    return pl.pallas_call(
        project_kernel,
        out_shape=jax.ShapeDtypeStruct((tok, model), BF16),
        in_specs=[pl.BlockSpec(memory_space=pltpu.VMEM)] * 2,
        out_specs=pl.BlockSpec(memory_space=pl.ANY),
        scratch_shapes=[
            pltpu.VMEM((tok, model), BF16),
            pltpu.SemaphoreType.DMA((tok // ROWS, model // TILE)),
        ],
        compiler_params=pltpu.CompilerParams(vmem_limit_bytes=20 * 1024 * 1024),
        name="project",
    )(normed, out_weight)


def solution(mesh):
    n_outer, n_inner = mesh.shape["outer"], mesh.shape["inner"]

    def on_device(queries, keys, values, norm_gain, out_weight):
        normed, weight = scan_and_norm(n_outer, n_inner, queries, keys, values, norm_gain, out_weight)
        return project(normed, weight)

    rows = P(("outer", "inner"), None)
    return jax.shard_map(
        on_device,
        mesh=mesh,
        in_specs=(rows, rows, rows, P(), P()),
        out_specs=rows,
        check_vma=False,
    )
```

```python
import functools

import jax
import jax.numpy as jnp
from jax import lax
from jax.experimental import pallas as pl
from jax.experimental.pallas import tpu as pltpu
from jax.sharding import PartitionSpec as P

H = 8
DH = 128
PAIRS = H // 2
PW = 2 * DH
C = 128
CHUNK = 256
ROWS = 256
TILE = 512
F32 = jnp.float32
BF16 = jnp.bfloat16
MESH = pl.DeviceIdType.MESH
ORDER = (1, 3, 2, 0)
PART = DH // 2
PARTS = (slice(0, PART), slice(PART, DH))


def scan_kernel(
    n_outer, n_inner, q_hbm, k_hbm, v_hbm, w_hbm, gain_hbm, normed, w,
    gain, q, k, v, pre, low, diag, averaging, local, pair_buf, chip, up_buf, zs, zb, zx, down_src, down_buf, fwd, pd,
    load_sem, w_sem, gain_sem, pair_send, pair_recv, up_send, up_recv, z_send, z_recv,
    down_send, down_recv, fwd_send, fwd_recv,
):
    tok = q.shape[0]
    blocks = tok // C
    groups = n_outer * n_inner // H
    rounds = (groups - 1).bit_length()
    me = lax.axis_index("outer") * n_inner + lax.axis_index("inner")
    group, place = me // H, me % H
    c, e = place // 2, place % 2

    def device(index):
        return (index // n_inner, index % n_inner)

    def remote(src, dst, send, recv, target):
        return pltpu.make_async_remote_copy(
            src_ref=src, dst_ref=dst, send_sem=send, recv_sem=recv,
            device_id=device(target), device_id_type=MESH,
        )

    partner = group * H + 2 * c + (1 - e)

    def mate(j):
        return group * H + 2 * j + e

    def cols(j, width):
        return pl.ds(pl.multiple_of(j * width, width), width)

    def load(which, hbm, vmem, j):
        return pltpu.make_async_copy(hbm.at[:, cols(j, PW)], vmem.at[:, cols(j, PW)], load_sem.at[which, j])

    barrier = pltpu.get_barrier_semaphore()

    def greet(target):
        pl.semaphore_signal(barrier, inc=1, device_id=device(target), device_id_type=MESH)

    greet(partner)
    for s in range(1, PAIRS):
        greet(mate((c + s) % PAIRS))
    expected = PAIRS
    for d in range(rounds):
        step = 1 << d
        up, down = group + step < groups, group >= step

        @pl.when(up)
        def _():
            greet(me + step * H)

        @pl.when(down)
        def _():
            greet(me - step * H)

        expected = expected + jnp.where(up, 1, 0) + jnp.where(down, 1, 0)

    for s in range(PAIRS):
        j = (c + ORDER[s]) % PAIRS
        load(0, k_hbm, k, j).start()
        load(1, v_hbm, v, j).start()
    for j in range(PAIRS):
        load(2, q_hbm, q, j).start()
    whole_w = pltpu.make_async_copy(w_hbm, w, w_sem)
    whole_w.start()
    whole_gain = pltpu.make_async_copy(gain_hbm, gain, gain_sem)
    whole_gain.start()
    diag[...] = jnp.zeros_like(diag)
    averaging[...] = jnp.zeros_like(averaging)
    for i in range(2):
        averaging[i * DH:(i + 1) * DH, i * DH:(i + 1) * DH] = jnp.full((DH, DH), 1.0 / DH, BF16)

    def pair_copy(j):
        return remote(local.at[2 * j + 1 - e], pair_buf.at[j], pair_send.at[j], pair_recv.at[j], partner)

    def part(p):
        return pl.ds(p * PART, PART)

    def up_copy(j, slot, p):
        return remote(
            chip.at[j, part(p)], up_buf.at[slot, part(p)], up_send.at[p, j], up_recv.at[p, slot], mate(j)
        )

    def chip_sum(s):
        j = (c + ORDER[s]) % PAIRS
        pair_copy(j).wait_recv()
        total = local[2 * j + e] + pair_buf[j]
        if ORDER[s]:
            chip[j] = total
            for p in range(2):
                up_copy(j, c, p).start()
        else:
            up_buf[c] = total

    for s in range(PAIRS):
        j = (c + ORDER[s]) % PAIRS
        load(0, k_hbm, k, j).wait()
        load(1, v_hbm, v, j).wait()
        sums = [None, None]
        for b in range(blocks):
            for half in range(2):
                at = (pl.ds(b * C, C), cols(2 * j + half, DH))
                own = lax.dot_general(k[at], v[at], (((0,), (0,)), ((), ())), preferred_element_type=F32)
                sums[half] = own if b == 0 else sums[half] + own
                if b + 1 < blocks:
                    low[2 * j + half, b] = sums[half].astype(BF16)
        local[2 * j] = sums[0]
        local[2 * j + 1] = sums[1]
        if s == 0:
            pl.semaphore_wait(barrier, expected)
        pair_copy(j).start()
        if s > 0:
            chip_sum(s - 1)
    chip_sum(PAIRS - 1)

    for j in range(PAIRS):
        load(2, q_hbm, q, j).wait()

    causal = lax.broadcasted_iota(jnp.int32, (C, C), 0) >= lax.broadcasted_iota(
        jnp.int32, (C, C), 1
    )

    def causal_part(h, _):
        left = []
        for b in range(blocks):
            at = (pl.ds(b * C, C), cols(h, DH))
            scores = lax.dot_general(q[at], k[at], (((1,), (1,)), ((), ())), preferred_element_type=F32)
            weights = jnp.where(causal, scores, 0.0).astype(BF16)
            left.append(jnp.concatenate([weights, q[at]], axis=1) if b else weights)
        for b in range(blocks):
            at = (pl.ds(b * C, C), cols(h, DH))
            right = jnp.concatenate([v[at], low[h, b - 1]], axis=0) if b else v[at]
            pre[at] = jnp.dot(left[b], right, preferred_element_type=F32)
        return 0

    done = 0

    def work(heads):
        nonlocal done
        until = min(H, done + heads)
        if until > done:
            lax.fori_loop(done, until, causal_part, 0)
        done = until

    def z_copy(d, target, p):
        return remote(zs.at[d, part(p)], zb.at[d, part(p)], z_send.at[p, d], z_recv.at[p, d], target)

    def z_start(d, p):
        @pl.when(group + (1 << d) < groups)
        def _():
            z_copy(d, me + (1 << d) * H, p).start()

    def z_take(d, p):
        rows = PARTS[p]

        @pl.when(group >= 1 << d)
        def _():
            z_copy(d, me - (1 << d) * H, p).wait_recv()
            zx[rows] = zx[rows] + zb[d, rows]

        if d + 1 < rounds:
            @pl.when(group >= 1 << d)
            def _():
                zs[d + 1, rows] = zs[d, rows] + zb[d, rows]

            @pl.when(group < 1 << d)
            def _():
                zs[d + 1, rows] = zs[d, rows]

    def down_copy(j, slot, p):
        return remote(
            down_src.at[j, part(p)], down_buf.at[slot, part(p)], down_send.at[p, j], down_recv.at[p, slot], mate(j)
        )

    def down_start(p):
        rows = PARTS[p]
        running = zx[rows]
        for i in range(PAIRS):
            down_src[i, rows] = running
            if i + 1 < PAIRS:
                running = running + up_buf[i, rows]
        for s in range(1, PAIRS):
            down_copy((c + s) % PAIRS, c, p).start()
        down_buf[c, rows] = down_src[c, rows]

    work(2)
    zx[...] = jnp.zeros_like(zx)
    for p in range(2):
        rows = PARTS[p]
        for s in range(1, PAIRS):
            j = (c + s) % PAIRS
            up_copy(j, j, p).wait_recv()
        zs[0, rows] = up_buf[0, rows] + up_buf[1, rows] + up_buf[2, rows] + up_buf[3, rows]
        z_start(0, p)
        work(1)
    for d in range(rounds):
        for p in range(2):
            z_take(d, p)
            if d + 1 < rounds:
                z_start(d + 1, p)
            else:
                down_start(p)
            work(1)
    work(H)

    def fwd_copy(j, p):
        return remote(fwd.at[j, part(p)], pd.at[j, part(p)], fwd_send.at[p, j], fwd_recv.at[p, j], partner)

    def spread(s, p):
        j = (c + s) % PAIRS
        rows = PARTS[p]
        if s:
            down_copy(j, j, p).wait_recv()
        first = down_buf[j, rows]
        fwd[j, rows] = jnp.where(e == 0, first + local[2 * j, rows], first)
        fwd_copy(j, p).start()
        at = pl.ds(pl.multiple_of(e * DH + p * PART, PART), PART)
        half = pl.ds(pl.multiple_of(e * DH, DH), DH)
        diag[s, at, half] = jnp.where(e == 1, first + pair_buf[j, rows], first).astype(BF16)

    def norm(s):
        j = (c + s) % PAIRS
        for p in range(2):
            fwd_copy(j, p).wait_recv()
        half = pl.ds(pl.multiple_of((1 - e) * DH, DH), DH)
        diag[s, half, half] = pd[j].astype(BF16)
        carried = diag[s]
        for b in range(tok // CHUNK):
            at = (pl.ds(b * CHUNK, CHUNK), cols(j, PW))
            attended = pre[at] + jnp.dot(q[at], carried, preferred_element_type=F32)
            mean_square = jnp.dot((attended * attended).astype(BF16), averaging[...], preferred_element_type=F32)
            scaled = attended * lax.rsqrt(mean_square + 1e-06) * gain[:, cols(j, PW)]
            normed[at] = scaled.astype(BF16)

    whole_gain.wait()
    for s in range(PAIRS):
        spread(s, 0)
    spread(0, 1)
    for s in range(1, PAIRS):
        spread(s, 1)
        norm(s - 1)
    norm(PAIRS - 1)
    whole_w.wait()

    for s in range(PAIRS):
        j = (c + s) % PAIRS
        pair_copy(j).wait_send()
        for p in range(2):
            fwd_copy(j, p).wait_send()
            if s:
                up_copy(j, c, p).wait_send()
                down_copy(j, c, p).wait_send()
    for d in range(rounds):
        @pl.when(group + (1 << d) < groups)
        def _():
            for p in range(2):
                z_copy(d, me + (1 << d) * H, p).wait_send()


def scan_and_norm(n_outer, n_inner, queries, keys, values, norm_gain, out_weight):
    tok, width = queries.shape
    rounds = max(1, (n_outer * n_inner // H - 1).bit_length())
    state = lambda count: pltpu.VMEM((count, DH, DH), F32)
    sems = lambda *shape: pltpu.SemaphoreType.DMA(shape)
    whole = pltpu.VMEM((tok, width), BF16)
    vmem = pl.BlockSpec(memory_space=pltpu.VMEM)
    held = [pltpu.with_memory_space_constraint(x, pltpu.HBM) for x in (queries, keys, values, out_weight, norm_gain.reshape(1, width))]
    return pl.pallas_call(
        functools.partial(scan_kernel, n_outer, n_inner),
        out_shape=(
            jax.ShapeDtypeStruct((tok, width), BF16),
            jax.ShapeDtypeStruct(out_weight.shape, BF16),
        ),
        in_specs=[pl.BlockSpec(memory_space=pl.ANY)] * 5,
        out_specs=(vmem, vmem),
        scratch_shapes=[
            pltpu.VMEM((1, width), F32), whole, whole, whole, pltpu.VMEM((tok, width), F32),
            pltpu.VMEM((H, max(1, tok // C - 1), DH, DH), BF16), pltpu.VMEM((PAIRS, PW, PW), BF16),
            pltpu.VMEM((PW, PW), BF16), state(H), state(PAIRS), state(PAIRS), state(PAIRS),
            state(rounds), state(rounds), pltpu.VMEM((DH, DH), F32),
            state(PAIRS), state(PAIRS), state(PAIRS), state(PAIRS),
            sems(3, PAIRS), pltpu.SemaphoreType.DMA, pltpu.SemaphoreType.DMA, sems(PAIRS), sems(PAIRS), sems(2, PAIRS), sems(2, PAIRS),
            sems(2, rounds), sems(2, rounds), sems(2, PAIRS), sems(2, PAIRS), sems(2, PAIRS), sems(2, PAIRS),
        ],
        compiler_params=pltpu.CompilerParams(
            collective_id=0, has_side_effects=True, vmem_limit_bytes=32 * 1024 * 1024
        ),
        name="scan_and_norm",
    )(*held)


def project_kernel(normed, w, out_hbm, out, out_sem):
    tok, model = out.shape
    copies = []
    for r in range(tok // ROWS):
        for n in range(model // TILE):
            rows, at = pl.ds(r * ROWS, ROWS), pl.ds(n * TILE, TILE)
            out[rows, at] = jnp.dot(normed[rows, :], w[:, at], preferred_element_type=F32).astype(BF16)
            copy = pltpu.make_async_copy(out.at[rows, at], out_hbm.at[rows, at], out_sem.at[r, n])
            copy.start()
            copies.append(copy)
    for copy in copies:
        copy.wait()


def project(normed, out_weight):
    tok, model = normed.shape[0], out_weight.shape[1]
    return pl.pallas_call(
        project_kernel,
        out_shape=jax.ShapeDtypeStruct((tok, model), BF16),
        in_specs=[pl.BlockSpec(memory_space=pltpu.VMEM)] * 2,
        out_specs=pl.BlockSpec(memory_space=pl.ANY),
        scratch_shapes=[
            pltpu.VMEM((tok, model), BF16),
            pltpu.SemaphoreType.DMA((tok // ROWS, model // TILE)),
        ],
        compiler_params=pltpu.CompilerParams(vmem_limit_bytes=20 * 1024 * 1024),
        name="project",
    )(normed, out_weight)


def solution(mesh):
    n_outer, n_inner = mesh.shape["outer"], mesh.shape["inner"]

    def on_device(queries, keys, values, norm_gain, out_weight):
        normed, weight = scan_and_norm(n_outer, n_inner, queries, keys, values, norm_gain, out_weight)
        return project(normed, weight)

    rows = P(("outer", "inner"), None)
    return jax.shard_map(
        on_device,
        mesh=mesh,
        in_specs=(rows, rows, rows, P(), P()),
        out_specs=rows,
        check_vma=False,
    )
```

```python
import functools

import jax
import jax.numpy as jnp
from jax import lax
from jax.experimental import pallas as pl
from jax.experimental.pallas import tpu as pltpu
from jax.sharding import PartitionSpec as P

H = 8
DH = 128
PAIRS = H // 2
PW = 2 * DH
C = 128
CHUNK = 256
ROWS = 256
TILE = 512
F32 = jnp.float32
BF16 = jnp.bfloat16
MESH = pl.DeviceIdType.MESH
ORDER = (1, 3, 2, 0)
PART = DH // 2
PARTS = (slice(0, PART), slice(PART, DH))


def scan_kernel(
    n_outer, n_inner, q_hbm, k_hbm, v_hbm, w_hbm, gain_hbm, normed, w,
    gain, q, k, v, pre, low, diag, averaging, local, pair_buf, chip, up_buf, zs, zb, zx, down_src, down_buf, fwd, pd,
    load_sem, w_sem, gain_sem, pair_send, pair_recv, up_send, up_recv, z_send, z_recv,
    down_send, down_recv, fwd_send, fwd_recv,
):
    tok = q.shape[0]
    blocks = tok // C
    groups = n_outer * n_inner // H
    rounds = (groups - 1).bit_length()
    me = lax.axis_index("outer") * n_inner + lax.axis_index("inner")
    group, place = me // H, me % H
    c, e = place // 2, place % 2

    def device(index):
        return (index // n_inner, index % n_inner)

    def remote(src, dst, send, recv, target):
        return pltpu.make_async_remote_copy(
            src_ref=src, dst_ref=dst, send_sem=send, recv_sem=recv,
            device_id=device(target), device_id_type=MESH,
        )

    partner = group * H + 2 * c + (1 - e)

    def mate(j):
        return group * H + 2 * j + e

    def cols(j, width):
        return pl.ds(pl.multiple_of(j * width, width), width)

    def load(which, hbm, vmem, j):
        return pltpu.make_async_copy(hbm.at[:, cols(j, PW)], vmem.at[:, cols(j, PW)], load_sem.at[which, j])

    barrier = pltpu.get_barrier_semaphore()

    def greet(target):
        pl.semaphore_signal(barrier, inc=1, device_id=device(target), device_id_type=MESH)

    greet(partner)
    for s in range(1, PAIRS):
        greet(mate((c + s) % PAIRS))
    expected = PAIRS
    for d in range(rounds):
        step = 1 << d
        up, down = group + step < groups, group >= step

        @pl.when(up)
        def _():
            greet(me + step * H)

        @pl.when(down)
        def _():
            greet(me - step * H)

        expected = expected + jnp.where(up, 1, 0) + jnp.where(down, 1, 0)

    for s in range(PAIRS):
        j = (c + ORDER[s]) % PAIRS
        load(0, k_hbm, k, j).start()
        load(1, v_hbm, v, j).start()
    diag[...] = jnp.zeros_like(diag)
    averaging[...] = jnp.zeros_like(averaging)
    for i in range(2):
        averaging[i * DH:(i + 1) * DH, i * DH:(i + 1) * DH] = jnp.full((DH, DH), 1.0 / DH, BF16)

    def pair_copy(j):
        return remote(local.at[2 * j + 1 - e], pair_buf.at[j], pair_send.at[j], pair_recv.at[j], partner)

    def part(p):
        return pl.ds(p * PART, PART)

    def up_copy(j, slot, p):
        return remote(
            chip.at[j, part(p)], up_buf.at[slot, part(p)], up_send.at[p, j], up_recv.at[p, slot], mate(j)
        )

    def chip_sum(s):
        j = (c + ORDER[s]) % PAIRS
        pair_copy(j).wait_recv()
        total = local[2 * j + e] + pair_buf[j]
        if ORDER[s]:
            chip[j] = total
            for p in range(2):
                up_copy(j, c, p).start()
        else:
            up_buf[c] = total

    for s in range(PAIRS):
        j = (c + ORDER[s]) % PAIRS
        load(0, k_hbm, k, j).wait()
        load(1, v_hbm, v, j).wait()
        sums = [None, None]
        for b in range(blocks):
            for half in range(2):
                at = (pl.ds(b * C, C), cols(2 * j + half, DH))
                own = lax.dot_general(k[at], v[at], (((0,), (0,)), ((), ())), preferred_element_type=F32)
                sums[half] = own if b == 0 else sums[half] + own
                if b + 1 < blocks:
                    low[2 * j + half, b] = sums[half].astype(BF16)
        local[2 * j] = sums[0]
        local[2 * j + 1] = sums[1]
        if s == 0:
            pl.semaphore_wait(barrier, expected)
        pair_copy(j).start()
        if s > 0:
            chip_sum(s - 1)
    for j in range(PAIRS):
        load(2, q_hbm, q, j).start()
    chip_sum(PAIRS - 1)
    whole_w = pltpu.make_async_copy(w_hbm, w, w_sem)
    whole_w.start()
    whole_gain = pltpu.make_async_copy(gain_hbm, gain, gain_sem)
    whole_gain.start()
    for j in range(PAIRS):
        load(2, q_hbm, q, j).wait()

    causal = lax.broadcasted_iota(jnp.int32, (C, C), 0) >= lax.broadcasted_iota(
        jnp.int32, (C, C), 1
    )

    def causal_part(h, _):
        left = []
        for b in range(blocks):
            at = (pl.ds(b * C, C), cols(h, DH))
            scores = lax.dot_general(q[at], k[at], (((1,), (1,)), ((), ())), preferred_element_type=F32)
            weights = jnp.where(causal, scores, 0.0).astype(BF16)
            left.append(jnp.concatenate([weights, q[at]], axis=1) if b else weights)
        for b in range(blocks):
            at = (pl.ds(b * C, C), cols(h, DH))
            right = jnp.concatenate([v[at], low[h, b - 1]], axis=0) if b else v[at]
            pre[at] = jnp.dot(left[b], right, preferred_element_type=F32)
        return 0

    done = 0

    def work(heads):
        nonlocal done
        until = min(H, done + heads)
        if until > done:
            lax.fori_loop(done, until, causal_part, 0)
        done = until

    def z_copy(d, target, p):
        return remote(zs.at[d, part(p)], zb.at[d, part(p)], z_send.at[p, d], z_recv.at[p, d], target)

    def z_start(d, p):
        @pl.when(group + (1 << d) < groups)
        def _():
            z_copy(d, me + (1 << d) * H, p).start()

    def z_take(d, p):
        rows = PARTS[p]

        @pl.when(group >= 1 << d)
        def _():
            z_copy(d, me - (1 << d) * H, p).wait_recv()
            zx[rows] = zx[rows] + zb[d, rows]

        if d + 1 < rounds:
            @pl.when(group >= 1 << d)
            def _():
                zs[d + 1, rows] = zs[d, rows] + zb[d, rows]

            @pl.when(group < 1 << d)
            def _():
                zs[d + 1, rows] = zs[d, rows]

    def down_copy(j, slot, p):
        return remote(
            down_src.at[j, part(p)], down_buf.at[slot, part(p)], down_send.at[p, j], down_recv.at[p, slot], mate(j)
        )

    def down_start(p):
        rows = PARTS[p]
        running = zx[rows]
        for i in range(PAIRS):
            down_src[i, rows] = running
            if i + 1 < PAIRS:
                running = running + up_buf[i, rows]
        for s in range(1, PAIRS):
            down_copy((c + s) % PAIRS, c, p).start()
        down_buf[c, rows] = down_src[c, rows]

    work(2)
    zx[...] = jnp.zeros_like(zx)
    for p in range(2):
        rows = PARTS[p]
        for s in range(1, PAIRS):
            j = (c + s) % PAIRS
            up_copy(j, j, p).wait_recv()
        zs[0, rows] = up_buf[0, rows] + up_buf[1, rows] + up_buf[2, rows] + up_buf[3, rows]
        z_start(0, p)
        work(1)
    for d in range(rounds):
        for p in range(2):
            z_take(d, p)
            if d + 1 < rounds:
                z_start(d + 1, p)
            else:
                down_start(p)
            work(1)
    work(H)

    def fwd_copy(j, p):
        return remote(fwd.at[j, part(p)], pd.at[j, part(p)], fwd_send.at[p, j], fwd_recv.at[p, j], partner)

    def spread(s, p):
        j = (c + s) % PAIRS
        rows = PARTS[p]
        if s:
            down_copy(j, j, p).wait_recv()
        first = down_buf[j, rows]
        fwd[j, rows] = jnp.where(e == 0, first + local[2 * j, rows], first)
        fwd_copy(j, p).start()
        at = pl.ds(pl.multiple_of(e * DH + p * PART, PART), PART)
        half = pl.ds(pl.multiple_of(e * DH, DH), DH)
        diag[s, at, half] = jnp.where(e == 1, first + pair_buf[j, rows], first).astype(BF16)

    def norm(s):
        j = (c + s) % PAIRS
        for p in range(2):
            fwd_copy(j, p).wait_recv()
        half = pl.ds(pl.multiple_of((1 - e) * DH, DH), DH)
        diag[s, half, half] = pd[j].astype(BF16)
        carried = diag[s]
        for b in range(tok // CHUNK):
            at = (pl.ds(b * CHUNK, CHUNK), cols(j, PW))
            attended = pre[at] + jnp.dot(q[at], carried, preferred_element_type=F32)
            mean_square = jnp.dot((attended * attended).astype(BF16), averaging[...], preferred_element_type=F32)
            scaled = attended * lax.rsqrt(mean_square + 1e-06) * gain[:, cols(j, PW)]
            normed[at] = scaled.astype(BF16)

    whole_gain.wait()
    for s in range(PAIRS):
        spread(s, 0)
    spread(0, 1)
    for s in range(1, PAIRS):
        spread(s, 1)
        norm(s - 1)
    norm(PAIRS - 1)
    whole_w.wait()

    for s in range(PAIRS):
        j = (c + s) % PAIRS
        pair_copy(j).wait_send()
        for p in range(2):
            fwd_copy(j, p).wait_send()
            if s:
                up_copy(j, c, p).wait_send()
                down_copy(j, c, p).wait_send()
    for d in range(rounds):
        @pl.when(group + (1 << d) < groups)
        def _():
            for p in range(2):
                z_copy(d, me + (1 << d) * H, p).wait_send()


def scan_and_norm(n_outer, n_inner, queries, keys, values, norm_gain, out_weight):
    tok, width = queries.shape
    rounds = max(1, (n_outer * n_inner // H - 1).bit_length())
    state = lambda count: pltpu.VMEM((count, DH, DH), F32)
    sems = lambda *shape: pltpu.SemaphoreType.DMA(shape)
    whole = pltpu.VMEM((tok, width), BF16)
    vmem = pl.BlockSpec(memory_space=pltpu.VMEM)
    held = [pltpu.with_memory_space_constraint(x, pltpu.HBM) for x in (queries, keys, values, out_weight, norm_gain.reshape(1, width))]
    return pl.pallas_call(
        functools.partial(scan_kernel, n_outer, n_inner),
        out_shape=(
            jax.ShapeDtypeStruct((tok, width), BF16),
            jax.ShapeDtypeStruct(out_weight.shape, BF16),
        ),
        in_specs=[pl.BlockSpec(memory_space=pl.ANY)] * 5,
        out_specs=(vmem, vmem),
        scratch_shapes=[
            pltpu.VMEM((1, width), F32), whole, whole, whole, pltpu.VMEM((tok, width), F32),
            pltpu.VMEM((H, max(1, tok // C - 1), DH, DH), BF16), pltpu.VMEM((PAIRS, PW, PW), BF16),
            pltpu.VMEM((PW, PW), BF16), state(H), state(PAIRS), state(PAIRS), state(PAIRS),
            state(rounds), state(rounds), pltpu.VMEM((DH, DH), F32),
            state(PAIRS), state(PAIRS), state(PAIRS), state(PAIRS),
            sems(3, PAIRS), pltpu.SemaphoreType.DMA, pltpu.SemaphoreType.DMA, sems(PAIRS), sems(PAIRS), sems(2, PAIRS), sems(2, PAIRS),
            sems(2, rounds), sems(2, rounds), sems(2, PAIRS), sems(2, PAIRS), sems(2, PAIRS), sems(2, PAIRS),
        ],
        compiler_params=pltpu.CompilerParams(
            collective_id=0, has_side_effects=True, vmem_limit_bytes=32 * 1024 * 1024
        ),
        name="scan_and_norm",
    )(*held)


def project_kernel(normed, w, out_hbm, out, out_sem):
    tok, model = out.shape
    copies = []
    for r in range(tok // ROWS):
        for n in range(model // TILE):
            rows, at = pl.ds(r * ROWS, ROWS), pl.ds(n * TILE, TILE)
            out[rows, at] = jnp.dot(normed[rows, :], w[:, at], preferred_element_type=F32).astype(BF16)
            copy = pltpu.make_async_copy(out.at[rows, at], out_hbm.at[rows, at], out_sem.at[r, n])
            copy.start()
            copies.append(copy)
    for copy in copies:
        copy.wait()


def project(normed, out_weight):
    tok, model = normed.shape[0], out_weight.shape[1]
    return pl.pallas_call(
        project_kernel,
        out_shape=jax.ShapeDtypeStruct((tok, model), BF16),
        in_specs=[pl.BlockSpec(memory_space=pltpu.VMEM)] * 2,
        out_specs=pl.BlockSpec(memory_space=pl.ANY),
        scratch_shapes=[
            pltpu.VMEM((tok, model), BF16),
            pltpu.SemaphoreType.DMA((tok // ROWS, model // TILE)),
        ],
        compiler_params=pltpu.CompilerParams(vmem_limit_bytes=20 * 1024 * 1024),
        name="project",
    )(normed, out_weight)


def solution(mesh):
    n_outer, n_inner = mesh.shape["outer"], mesh.shape["inner"]

    def on_device(queries, keys, values, norm_gain, out_weight):
        normed, weight = scan_and_norm(n_outer, n_inner, queries, keys, values, norm_gain, out_weight)
        return project(normed, weight)

    rows = P(("outer", "inner"), None)
    return jax.shard_map(
        on_device,
        mesh=mesh,
        in_specs=(rows, rows, rows, P(), P()),
        out_specs=rows,
        check_vma=False,
    )
```

```python
import functools

import jax
import jax.numpy as jnp
from jax import lax
from jax.experimental import pallas as pl
from jax.experimental.pallas import tpu as pltpu
from jax.sharding import PartitionSpec as P

H = 8
DH = 128
PAIRS = H // 2
PW = 2 * DH
C = 128
CHUNK = 256
ROWS = 256
TILE = 512
F32 = jnp.float32
BF16 = jnp.bfloat16
MESH = pl.DeviceIdType.MESH
PART = DH // 2
PARTS = (slice(0, PART), slice(PART, DH))


def scan_kernel(
    n_outer, n_inner, q_hbm, k_hbm, v_hbm, w_hbm, gain_hbm, normed, w,
    gain, q, k, v, pre, low, diag, averaging, local, pair_buf, chip, up_buf, zs, zb, zx, down_src, down_buf, fwd, pd,
    load_sem, w_sem, gain_sem, pair_send, pair_recv, up_send, up_recv, z_send, z_recv,
    down_send, down_recv, fwd_send, fwd_recv,
):
    tok = q.shape[0]
    blocks = tok // C
    groups = n_outer * n_inner // H
    rounds = (groups - 1).bit_length()
    me = lax.axis_index("outer") * n_inner + lax.axis_index("inner")
    group, place = me // H, me % H
    c, e = place // 2, place % 2

    def device(index):
        return (index // n_inner, index % n_inner)

    def remote(src, dst, send, recv, target):
        return pltpu.make_async_remote_copy(
            src_ref=src, dst_ref=dst, send_sem=send, recv_sem=recv,
            device_id=device(target), device_id_type=MESH,
        )

    partner = group * H + 2 * c + (1 - e)

    def mate(j):
        return group * H + 2 * j + e

    def cols(j, width):
        return pl.ds(pl.multiple_of(j * width, width), width)

    def load(which, hbm, vmem, j):
        return pltpu.make_async_copy(hbm.at[:, cols(j, PW)], vmem.at[:, cols(j, PW)], load_sem.at[which, j])

    barrier = pltpu.get_barrier_semaphore()

    def greet(target):
        pl.semaphore_signal(barrier, inc=1, device_id=device(target), device_id_type=MESH)

    greet(partner)
    for s in range(1, PAIRS):
        greet(mate((c + s) % PAIRS))
    expected = PAIRS
    for d in range(rounds):
        step = 1 << d
        up, down = group + step < groups, group >= step

        @pl.when(up)
        def _():
            greet(me + step * H)

        @pl.when(down)
        def _():
            greet(me - step * H)

        expected = expected + jnp.where(up, 1, 0) + jnp.where(down, 1, 0)

    for s in range(PAIRS):
        j = (c + s + 1) % PAIRS
        load(0, k_hbm, k, j).start()
        load(1, v_hbm, v, j).start()
    diag[...] = jnp.zeros_like(diag)
    averaging[...] = jnp.zeros_like(averaging)
    for i in range(2):
        averaging[i * DH:(i + 1) * DH, i * DH:(i + 1) * DH] = jnp.full((DH, DH), 1.0 / DH, BF16)

    def pair_copy(j):
        return remote(local.at[2 * j + 1 - e], pair_buf.at[j], pair_send.at[j], pair_recv.at[j], partner)

    def part(p):
        return pl.ds(p * PART, PART)

    def up_copy(j, slot, p):
        return remote(
            chip.at[j, part(p)], up_buf.at[slot, part(p)], up_send.at[p, j], up_recv.at[p, slot], mate(j)
        )

    def first_pass(s, _):
        @pl.when(s < PAIRS)
        def _():
            j = (c + s + 1) % PAIRS
            load(0, k_hbm, k, j).wait()
            load(1, v_hbm, v, j).wait()
            sums = [None, None]
            for b in range(blocks):
                for half in range(2):
                    at = (pl.ds(b * C, C), cols(2 * j + half, DH))
                    own = lax.dot_general(k[at], v[at], (((0,), (0,)), ((), ())), preferred_element_type=F32)
                    sums[half] = own if b == 0 else sums[half] + own
                    if b + 1 < blocks:
                        low[2 * j + half, b] = sums[half].astype(BF16)
            local[2 * j] = sums[0]
            local[2 * j + 1] = sums[1]
            pair_copy(j).start()

        @pl.when(s > 0)
        def _():
            j = (c + s) % PAIRS
            pair_copy(j).wait_recv()
            total = local[2 * j + e] + pair_buf[j]

            @pl.when(s < PAIRS)
            def _():
                chip[j] = total
                for p in range(2):
                    up_copy(j, c, p).start()

            @pl.when(s == PAIRS)
            def _():
                up_buf[c] = total

        return 0

    for j in range(PAIRS):
        load(2, q_hbm, q, j).start()
    pl.semaphore_wait(barrier, expected)
    lax.fori_loop(0, PAIRS + 1, first_pass, 0)
    whole_w = pltpu.make_async_copy(w_hbm, w, w_sem)
    whole_w.start()
    whole_gain = pltpu.make_async_copy(gain_hbm, gain, gain_sem)
    whole_gain.start()
    for j in range(PAIRS):
        load(2, q_hbm, q, j).wait()

    causal = lax.broadcasted_iota(jnp.int32, (C, C), 0) >= lax.broadcasted_iota(
        jnp.int32, (C, C), 1
    )

    def causal_part(h):
        left = []
        for b in range(blocks):
            at = (pl.ds(b * C, C), cols(h, DH))
            scores = lax.dot_general(q[at], k[at], (((1,), (1,)), ((), ())), preferred_element_type=F32)
            weights = jnp.where(causal, scores, 0.0).astype(BF16)
            left.append(jnp.concatenate([weights, q[at]], axis=1) if b else weights)
        for b in range(blocks):
            at = (pl.ds(b * C, C), cols(h, DH))
            right = jnp.concatenate([v[at], low[h, b - 1]], axis=0) if b else v[at]
            pre[at] = jnp.dot(left[b], right, preferred_element_type=F32)

    def z_copy(d, target, p):
        return remote(zs.at[d, part(p)], zb.at[d, part(p)], z_send.at[p, d], z_recv.at[p, d], target)

    def z_start(d, p):
        @pl.when(group + (1 << d) < groups)
        def _():
            z_copy(d, me + (1 << d) * H, p).start()

    def z_take(d, p):
        rows = PARTS[p]

        @pl.when(group >= 1 << d)
        def _():
            z_copy(d, me - (1 << d) * H, p).wait_recv()
            zx[rows] = zx[rows] + zb[d, rows]

        if d + 1 < rounds:
            @pl.when(group >= 1 << d)
            def _():
                zs[d + 1, rows] = zs[d, rows] + zb[d, rows]

            @pl.when(group < 1 << d)
            def _():
                zs[d + 1, rows] = zs[d, rows]

    def down_copy(j, slot, p):
        return remote(
            down_src.at[j, part(p)], down_buf.at[slot, part(p)], down_send.at[p, j], down_recv.at[p, slot], mate(j)
        )

    def down_start(p):
        rows = PARTS[p]
        running = zx[rows]
        for i in range(PAIRS):
            down_src[i, rows] = running
            if i + 1 < PAIRS:
                running = running + up_buf[i, rows]
        for s in range(1, PAIRS):
            down_copy((c + s) % PAIRS, c, p).start()
        down_buf[c, rows] = down_src[c, rows]

    def up_take(p):
        rows = PARTS[p]
        for s in range(1, PAIRS):
            j = (c + s) % PAIRS
            up_copy(j, j, p).wait_recv()
        zs[0, rows] = up_buf[0, rows] + up_buf[1, rows] + up_buf[2, rows] + up_buf[3, rows]

    def exchange(i):
        for p in range(2):
            if i == 0:
                up_take(p)
            else:
                z_take(i - 1, p)
            if i < rounds:
                z_start(i, p)
            else:
                down_start(p)

    zx[...] = jnp.zeros_like(zx)
    stride = 2 if rounds < 4 else 1

    def tick(h, _):
        causal_part(h)
        for i in range(rounds + 1):
            @pl.when(h == min(H - 1, 1 + i * stride))
            def _():
                exchange(i)
        return 0

    lax.fori_loop(0, H, tick, 0)

    def fwd_copy(j, p):
        return remote(fwd.at[j, part(p)], pd.at[j, part(p)], fwd_send.at[p, j], fwd_recv.at[p, j], partner)

    def spread(s, p):
        j = (c + s) % PAIRS
        rows = PARTS[p]

        @pl.when(s > 0)
        def _():
            down_copy(j, j, p).wait_recv()

        first = down_buf[j, rows]
        fwd[j, rows] = jnp.where(e == 0, first + local[2 * j, rows], first)
        fwd_copy(j, p).start()
        at = pl.ds(pl.multiple_of(e * DH + p * PART, PART), PART)
        half = pl.ds(pl.multiple_of(e * DH, DH), DH)
        diag[s, at, half] = jnp.where(e == 1, first + pair_buf[j, rows], first).astype(BF16)

    def norm(s):
        j = (c + s) % PAIRS
        for p in range(2):
            fwd_copy(j, p).wait_recv()
        half = pl.ds(pl.multiple_of((1 - e) * DH, DH), DH)
        diag[s, half, half] = pd[j].astype(BF16)
        carried = diag[s]
        for b in range(tok // CHUNK):
            at = (pl.ds(b * CHUNK, CHUNK), cols(j, PW))
            attended = pre[at] + jnp.dot(q[at], carried, preferred_element_type=F32)
            mean_square = jnp.dot((attended * attended).astype(BF16), averaging[...], preferred_element_type=F32)
            scaled = attended * lax.rsqrt(mean_square + 1e-06) * gain[:, cols(j, PW)]
            normed[at] = scaled.astype(BF16)

    whole_gain.wait()
    def take_first(s, _):
        spread(s, 0)
        return 0

    def take_second(s, _):
        @pl.when(s < PAIRS)
        def _():
            spread(s, 1)

        @pl.when(s > 0)
        def _():
            norm(s - 1)

        return 0

    lax.fori_loop(0, PAIRS, take_first, 0)
    lax.fori_loop(0, PAIRS + 1, take_second, 0)
    whole_w.wait()

    for s in range(PAIRS):
        j = (c + s) % PAIRS
        pair_copy(j).wait_send()
        for p in range(2):
            fwd_copy(j, p).wait_send()
            if s:
                up_copy(j, c, p).wait_send()
                down_copy(j, c, p).wait_send()
    for d in range(rounds):
        @pl.when(group + (1 << d) < groups)
        def _():
            for p in range(2):
                z_copy(d, me + (1 << d) * H, p).wait_send()


def scan_and_norm(n_outer, n_inner, queries, keys, values, norm_gain, out_weight):
    tok, width = queries.shape
    rounds = max(1, (n_outer * n_inner // H - 1).bit_length())
    state = lambda count: pltpu.VMEM((count, DH, DH), F32)
    sems = lambda *shape: pltpu.SemaphoreType.DMA(shape)
    whole = pltpu.VMEM((tok, width), BF16)
    vmem = pl.BlockSpec(memory_space=pltpu.VMEM)
    held = [pltpu.with_memory_space_constraint(x, pltpu.HBM) for x in (queries, keys, values, out_weight, norm_gain.reshape(1, width))]
    return pl.pallas_call(
        functools.partial(scan_kernel, n_outer, n_inner),
        out_shape=(
            jax.ShapeDtypeStruct((tok, width), BF16),
            jax.ShapeDtypeStruct(out_weight.shape, BF16),
        ),
        in_specs=[pl.BlockSpec(memory_space=pl.ANY)] * 5,
        out_specs=(vmem, vmem),
        scratch_shapes=[
            pltpu.VMEM((1, width), F32), whole, whole, whole, pltpu.VMEM((tok, width), F32),
            pltpu.VMEM((H, max(1, tok // C - 1), DH, DH), BF16), pltpu.VMEM((PAIRS, PW, PW), BF16),
            pltpu.VMEM((PW, PW), BF16), state(H), state(PAIRS), state(PAIRS), state(PAIRS),
            state(rounds), state(rounds), pltpu.VMEM((DH, DH), F32),
            state(PAIRS), state(PAIRS), state(PAIRS), state(PAIRS),
            sems(3, PAIRS), pltpu.SemaphoreType.DMA, pltpu.SemaphoreType.DMA, sems(PAIRS), sems(PAIRS), sems(2, PAIRS), sems(2, PAIRS),
            sems(2, rounds), sems(2, rounds), sems(2, PAIRS), sems(2, PAIRS), sems(2, PAIRS), sems(2, PAIRS),
        ],
        compiler_params=pltpu.CompilerParams(
            collective_id=0, has_side_effects=True, vmem_limit_bytes=32 * 1024 * 1024
        ),
        name="scan_and_norm",
    )(*held)


def project_kernel(normed, w, out_hbm, out, out_sem):
    tok, model = out.shape
    chunks = tok // ROWS

    def store(r):
        rows = pl.ds(pl.multiple_of(r * ROWS, ROWS), ROWS)
        return pltpu.make_async_copy(out.at[rows, :], out_hbm.at[rows, :], out_sem.at[r])

    def chunk(r, _):
        rows = pl.ds(pl.multiple_of(r * ROWS, ROWS), ROWS)
        for n in range(model // TILE):
            at = pl.ds(n * TILE, TILE)
            out[rows, at] = jnp.dot(normed[rows, :], w[:, at], preferred_element_type=F32).astype(BF16)
        store(r).start()
        return 0

    lax.fori_loop(0, chunks, chunk, 0)
    for r in range(chunks):
        store(r).wait()


def project(normed, out_weight):
    tok, model = normed.shape[0], out_weight.shape[1]
    return pl.pallas_call(
        project_kernel,
        out_shape=jax.ShapeDtypeStruct((tok, model), BF16),
        in_specs=[pl.BlockSpec(memory_space=pltpu.VMEM)] * 2,
        out_specs=pl.BlockSpec(memory_space=pl.ANY),
        scratch_shapes=[
            pltpu.VMEM((tok, model), BF16),
            pltpu.SemaphoreType.DMA((tok // ROWS,)),
        ],
        compiler_params=pltpu.CompilerParams(vmem_limit_bytes=20 * 1024 * 1024),
        name="project",
    )(normed, out_weight)


def solution(mesh):
    n_outer, n_inner = mesh.shape["outer"], mesh.shape["inner"]

    def on_device(queries, keys, values, norm_gain, out_weight):
        normed, weight = scan_and_norm(n_outer, n_inner, queries, keys, values, norm_gain, out_weight)
        return project(normed, weight)

    rows = P(("outer", "inner"), None)
    return jax.shard_map(
        on_device,
        mesh=mesh,
        in_specs=(rows, rows, rows, P(), P()),
        out_specs=rows,
        check_vma=False,
    )
```

```python
import functools

import jax
import jax.numpy as jnp
from jax import lax
from jax.experimental import pallas as pl
from jax.experimental.pallas import tpu as pltpu
from jax.sharding import PartitionSpec as P

H = 8
DH = 128
PAIRS = H // 2
PW = 2 * DH
C = 128
CHUNK = 256
ROWS = 256
TILE = 512
F32 = jnp.float32
BF16 = jnp.bfloat16
MESH = pl.DeviceIdType.MESH
ORDER = (1, 3, 2, 0)
PART = DH // 2
PARTS = (slice(0, PART), slice(PART, DH))


def scan_kernel(
    n_outer, n_inner, q_hbm, k_hbm, v_hbm, w_hbm, gain_hbm, normed, w,
    gain, q, k, v, pre, diag, averaging, local, pair_buf, chip, up_buf, zs, zb, zx, down_src, down_buf, fwd, pd,
    load_sem, w_sem, gain_sem, pair_send, pair_recv, up_send, up_recv, z_send, z_recv,
    down_send, down_recv, fwd_send, fwd_recv,
):
    tok = q.shape[0]
    blocks = tok // C
    groups = n_outer * n_inner // H
    rounds = (groups - 1).bit_length()
    me = lax.axis_index("outer") * n_inner + lax.axis_index("inner")
    group, place = me // H, me % H
    c, e = place // 2, place % 2

    def device(index):
        return (index // n_inner, index % n_inner)

    def remote(src, dst, send, recv, target):
        return pltpu.make_async_remote_copy(
            src_ref=src, dst_ref=dst, send_sem=send, recv_sem=recv,
            device_id=device(target), device_id_type=MESH,
        )

    partner = group * H + 2 * c + (1 - e)

    def mate(j):
        return group * H + 2 * j + e

    def cols(j, width):
        return pl.ds(pl.multiple_of(j * width, width), width)

    def load(which, hbm, vmem, j):
        return pltpu.make_async_copy(hbm.at[:, cols(j, PW)], vmem.at[:, cols(j, PW)], load_sem.at[which, j])

    barrier = pltpu.get_barrier_semaphore()

    def greet(target):
        pl.semaphore_signal(barrier, inc=1, device_id=device(target), device_id_type=MESH)

    greet(partner)
    for s in range(1, PAIRS):
        greet(mate((c + s) % PAIRS))
    expected = PAIRS
    for d in range(rounds):
        step = 1 << d
        up, down = group + step < groups, group >= step

        @pl.when(up)
        def _():
            greet(me + step * H)

        @pl.when(down)
        def _():
            greet(me - step * H)

        expected = expected + jnp.where(up, 1, 0) + jnp.where(down, 1, 0)

    for s in range(PAIRS):
        j = (c + ORDER[s]) % PAIRS
        load(0, k_hbm, k, j).start()
        load(1, v_hbm, v, j).start()
    diag[...] = jnp.zeros_like(diag)
    averaging[...] = jnp.zeros_like(averaging)
    for i in range(2):
        averaging[i * DH:(i + 1) * DH, i * DH:(i + 1) * DH] = jnp.full((DH, DH), 1.0 / DH, BF16)

    def pair_copy(j):
        return remote(local.at[2 * j + 1 - e], pair_buf.at[j], pair_send.at[j], pair_recv.at[j], partner)

    def part(p):
        return pl.ds(p * PART, PART)

    def up_copy(j, slot, p):
        return remote(
            chip.at[j, part(p)], up_buf.at[slot, part(p)], up_send.at[p, j], up_recv.at[p, slot], mate(j)
        )

    def chip_sum(s):
        j = (c + ORDER[s]) % PAIRS
        pair_copy(j).wait_recv()
        total = local[2 * j + e] + pair_buf[j]
        if ORDER[s]:
            chip[j] = total
            for p in range(2):
                up_copy(j, c, p).start()
        else:
            up_buf[c] = total

    for s in range(PAIRS):
        j = (c + ORDER[s]) % PAIRS
        load(0, k_hbm, k, j).wait()
        load(1, v_hbm, v, j).wait()
        both = lax.dot_general(
            k[:, cols(j, PW)], v[:, cols(j, PW)], (((0,), (0,)), ((), ())), preferred_element_type=F32
        )
        local[2 * j] = both[:DH, :DH]
        local[2 * j + 1] = both[DH:, DH:]
        if s == 0:
            pl.semaphore_wait(barrier, expected)
        pair_copy(j).start()
        if s > 0:
            chip_sum(s - 1)
    for j in range(PAIRS):
        load(2, q_hbm, q, j).start()
    chip_sum(PAIRS - 1)
    whole_w = pltpu.make_async_copy(w_hbm, w, w_sem)
    whole_w.start()
    whole_gain = pltpu.make_async_copy(gain_hbm, gain, gain_sem)
    whole_gain.start()
    for j in range(PAIRS):
        load(2, q_hbm, q, j).wait()

    causal = lax.broadcasted_iota(jnp.int32, (C, C), 0) >= lax.broadcasted_iota(
        jnp.int32, (C, C), 1
    )

    def causal_part(h, _):
        left = []
        for b in range(blocks):
            at = (pl.ds(b * C, C), cols(h, DH))
            scores = lax.dot_general(q[at], k[at], (((1,), (1,)), ((), ())), preferred_element_type=F32)
            weights = jnp.where(causal, scores, 0.0).astype(BF16)
            left.append(jnp.concatenate([weights, q[at]], axis=1) if b else weights)
        states = []
        for b in range(blocks - 1):
            at = (pl.ds(b * C, C), cols(h, DH))
            own = lax.dot_general(k[at], v[at], (((0,), (0,)), ((), ())), preferred_element_type=F32)
            states.append(states[-1] + own if b else own)
        for b in range(blocks):
            at = (pl.ds(b * C, C), cols(h, DH))
            right = jnp.concatenate([v[at], states[b - 1].astype(BF16)], axis=0) if b else v[at]
            pre[at] = jnp.dot(left[b], right, preferred_element_type=F32)
        return 0

    done = 0

    def work(heads):
        nonlocal done
        until = min(H, done + heads)
        if until > done:
            lax.fori_loop(done, until, causal_part, 0)
        done = until

    def z_copy(d, target, p):
        return remote(zs.at[d, part(p)], zb.at[d, part(p)], z_send.at[p, d], z_recv.at[p, d], target)

    def z_start(d, p):
        @pl.when(group + (1 << d) < groups)
        def _():
            z_copy(d, me + (1 << d) * H, p).start()

    def z_take(d, p):
        rows = PARTS[p]

        @pl.when(group >= 1 << d)
        def _():
            z_copy(d, me - (1 << d) * H, p).wait_recv()
            zx[rows] = zx[rows] + zb[d, rows]

        if d + 1 < rounds:
            @pl.when(group >= 1 << d)
            def _():
                zs[d + 1, rows] = zs[d, rows] + zb[d, rows]

            @pl.when(group < 1 << d)
            def _():
                zs[d + 1, rows] = zs[d, rows]

    def down_copy(j, slot, p):
        return remote(
            down_src.at[j, part(p)], down_buf.at[slot, part(p)], down_send.at[p, j], down_recv.at[p, slot], mate(j)
        )

    def down_start(p):
        rows = PARTS[p]
        running = zx[rows]
        for i in range(PAIRS):
            down_src[i, rows] = running
            if i + 1 < PAIRS:
                running = running + up_buf[i, rows]
        for s in range(1, PAIRS):
            down_copy((c + s) % PAIRS, c, p).start()
        down_buf[c, rows] = down_src[c, rows]

    work(2)
    zx[...] = jnp.zeros_like(zx)
    for p in range(2):
        rows = PARTS[p]
        for s in range(1, PAIRS):
            j = (c + s) % PAIRS
            up_copy(j, j, p).wait_recv()
        zs[0, rows] = up_buf[0, rows] + up_buf[1, rows] + up_buf[2, rows] + up_buf[3, rows]
        z_start(0, p)
    work(2)
    for d in range(rounds):
        for p in range(2):
            z_take(d, p)
            if d + 1 < rounds:
                z_start(d + 1, p)
            else:
                down_start(p)
        if d + 1 < rounds:
            work(3)
    work(H)

    def fwd_copy(j, p):
        return remote(fwd.at[j, part(p)], pd.at[j, part(p)], fwd_send.at[p, j], fwd_recv.at[p, j], partner)

    def spread(s, p):
        j = (c + s) % PAIRS
        rows = PARTS[p]
        if s:
            down_copy(j, j, p).wait_recv()
        first = down_buf[j, rows]
        fwd[j, rows] = jnp.where(e == 0, first + local[2 * j, rows], first)
        fwd_copy(j, p).start()
        at = pl.ds(pl.multiple_of(e * DH + p * PART, PART), PART)
        half = pl.ds(pl.multiple_of(e * DH, DH), DH)
        diag[s, at, half] = jnp.where(e == 1, first + pair_buf[j, rows], first).astype(BF16)

    def norm(s):
        j = (c + s) % PAIRS
        for p in range(2):
            fwd_copy(j, p).wait_recv()
        half = pl.ds(pl.multiple_of((1 - e) * DH, DH), DH)
        diag[s, half, half] = pd[j].astype(BF16)
        carried = diag[s]
        for b in range(tok // CHUNK):
            at = (pl.ds(b * CHUNK, CHUNK), cols(j, PW))
            attended = pre[at] + jnp.dot(q[at], carried, preferred_element_type=F32)
            mean_square = jnp.dot((attended * attended).astype(BF16), averaging[...], preferred_element_type=F32)
            scaled = attended * lax.rsqrt(mean_square + 1e-06) * gain[:, cols(j, PW)]
            normed[at] = scaled.astype(BF16)

    whole_gain.wait()
    for s in range(PAIRS):
        spread(s, 0)
    spread(0, 1)
    for s in range(1, PAIRS):
        spread(s, 1)
        norm(s - 1)
    norm(PAIRS - 1)
    whole_w.wait()

    for s in range(PAIRS):
        j = (c + s) % PAIRS
        pair_copy(j).wait_send()
        for p in range(2):
            fwd_copy(j, p).wait_send()
            if s:
                up_copy(j, c, p).wait_send()
                down_copy(j, c, p).wait_send()
    for d in range(rounds):
        @pl.when(group + (1 << d) < groups)
        def _():
            for p in range(2):
                z_copy(d, me + (1 << d) * H, p).wait_send()


def scan_and_norm(n_outer, n_inner, queries, keys, values, norm_gain, out_weight):
    tok, width = queries.shape
    rounds = max(1, (n_outer * n_inner // H - 1).bit_length())
    state = lambda count: pltpu.VMEM((count, DH, DH), F32)
    sems = lambda *shape: pltpu.SemaphoreType.DMA(shape)
    whole = pltpu.VMEM((tok, width), BF16)
    vmem = pl.BlockSpec(memory_space=pltpu.VMEM)
    held = [pltpu.with_memory_space_constraint(x, pltpu.HBM) for x in (queries, keys, values, out_weight, norm_gain.reshape(1, width))]
    return pl.pallas_call(
        functools.partial(scan_kernel, n_outer, n_inner),
        out_shape=(
            jax.ShapeDtypeStruct((tok, width), BF16),
            jax.ShapeDtypeStruct(out_weight.shape, BF16),
        ),
        in_specs=[pl.BlockSpec(memory_space=pl.ANY)] * 5,
        out_specs=(vmem, vmem),
        scratch_shapes=[
            pltpu.VMEM((1, width), F32), whole, whole, whole, pltpu.VMEM((tok, width), F32),
            pltpu.VMEM((PAIRS, PW, PW), BF16),
            pltpu.VMEM((PW, PW), BF16), state(H), state(PAIRS), state(PAIRS), state(PAIRS),
            state(rounds), state(rounds), pltpu.VMEM((DH, DH), F32),
            state(PAIRS), state(PAIRS), state(PAIRS), state(PAIRS),
            sems(3, PAIRS), pltpu.SemaphoreType.DMA, pltpu.SemaphoreType.DMA, sems(PAIRS), sems(PAIRS), sems(2, PAIRS), sems(2, PAIRS),
            sems(2, rounds), sems(2, rounds), sems(2, PAIRS), sems(2, PAIRS), sems(2, PAIRS), sems(2, PAIRS),
        ],
        compiler_params=pltpu.CompilerParams(
            collective_id=0, has_side_effects=True, vmem_limit_bytes=32 * 1024 * 1024
        ),
        name="scan_and_norm",
    )(*held)


def project_kernel(normed, w, out_hbm, out, out_sem):
    tok, model = out.shape
    copies = []
    for r in range(tok // ROWS):
        for n in range(model // TILE):
            rows, at = pl.ds(r * ROWS, ROWS), pl.ds(n * TILE, TILE)
            out[rows, at] = jnp.dot(normed[rows, :], w[:, at], preferred_element_type=F32).astype(BF16)
            copy = pltpu.make_async_copy(out.at[rows, at], out_hbm.at[rows, at], out_sem.at[r, n])
            copy.start()
            copies.append(copy)
    for copy in copies:
        copy.wait()


def project(normed, out_weight):
    tok, model = normed.shape[0], out_weight.shape[1]
    return pl.pallas_call(
        project_kernel,
        out_shape=jax.ShapeDtypeStruct((tok, model), BF16),
        in_specs=[pl.BlockSpec(memory_space=pltpu.VMEM)] * 2,
        out_specs=pl.BlockSpec(memory_space=pl.ANY),
        scratch_shapes=[
            pltpu.VMEM((tok, model), BF16),
            pltpu.SemaphoreType.DMA((tok // ROWS, model // TILE)),
        ],
        compiler_params=pltpu.CompilerParams(vmem_limit_bytes=20 * 1024 * 1024),
        name="project",
    )(normed, out_weight)


def solution(mesh):
    n_outer, n_inner = mesh.shape["outer"], mesh.shape["inner"]

    def on_device(queries, keys, values, norm_gain, out_weight):
        normed, weight = scan_and_norm(n_outer, n_inner, queries, keys, values, norm_gain, out_weight)
        return project(normed, weight)

    rows = P(("outer", "inner"), None)
    return jax.shard_map(
        on_device,
        mesh=mesh,
        in_specs=(rows, rows, rows, P(), P()),
        out_specs=rows,
        check_vma=False,
    )
```

```python
import functools

import jax
import jax.numpy as jnp
from jax import lax
from jax.experimental import pallas as pl
from jax.experimental.pallas import tpu as pltpu
from jax.sharding import PartitionSpec as P

H = 8
DH = 128
PAIRS = H // 2
PW = 2 * DH
C = 128
CHUNK = 256
ROWS = 256
TILE = 512
F32 = jnp.float32
BF16 = jnp.bfloat16
MESH = pl.DeviceIdType.MESH
ORDER = (1, 3, 2, 0)
PART = DH // 2
PARTS = (slice(0, PART), slice(PART, DH))


def scan_kernel(
    n_outer, n_inner, q_hbm, k_hbm, v_hbm, w_hbm, gain_hbm, normed, w,
    gain, q, k, v, pre, low, diag, averaging, local, pair_buf, chip, up_buf, zs, zb, zx, down_src, down_buf, fwd, pd,
    load_sem, w_sem, gain_sem, pair_send, pair_recv, up_send, up_recv, z_send, z_recv,
    down_send, down_recv, fwd_send, fwd_recv,
):
    tok = q.shape[0]
    blocks = tok // C
    groups = n_outer * n_inner // H
    rounds = (groups - 1).bit_length()
    me = lax.axis_index("outer") * n_inner + lax.axis_index("inner")
    group, place = me // H, me % H
    c, e = place // 2, place % 2

    def device(index):
        return (index // n_inner, index % n_inner)

    def remote(src, dst, send, recv, target):
        return pltpu.make_async_remote_copy(
            src_ref=src, dst_ref=dst, send_sem=send, recv_sem=recv,
            device_id=device(target), device_id_type=MESH,
        )

    partner = group * H + 2 * c + (1 - e)

    def mate(j):
        return group * H + 2 * j + e

    def cols(j, width):
        return pl.ds(pl.multiple_of(j * width, width), width)

    def load(which, hbm, vmem, j):
        return pltpu.make_async_copy(hbm.at[:, cols(j, PW)], vmem.at[:, cols(j, PW)], load_sem.at[which, j])

    barrier = pltpu.get_barrier_semaphore()

    def greet(target):
        pl.semaphore_signal(barrier, inc=1, device_id=device(target), device_id_type=MESH)

    greet(partner)
    for s in range(1, PAIRS):
        greet(mate((c + s) % PAIRS))
    expected = PAIRS
    for d in range(rounds):
        step = 1 << d
        up, down = group + step < groups, group >= step

        @pl.when(up)
        def _():
            greet(me + step * H)

        @pl.when(down)
        def _():
            greet(me - step * H)

        expected = expected + jnp.where(up, 1, 0) + jnp.where(down, 1, 0)

    for s in range(PAIRS):
        j = (c + ORDER[s]) % PAIRS
        load(0, k_hbm, k, j).start()
        load(1, v_hbm, v, j).start()
    diag[...] = jnp.zeros_like(diag)
    averaging[...] = jnp.zeros_like(averaging)
    for i in range(2):
        averaging[i * DH:(i + 1) * DH, i * DH:(i + 1) * DH] = jnp.full((DH, DH), 1.0 / DH, BF16)

    def pair_copy(j):
        return remote(local.at[2 * j + 1 - e], pair_buf.at[j], pair_send.at[j], pair_recv.at[j], partner)

    def part(p):
        return pl.ds(p * PART, PART)

    def up_copy(j, slot, p):
        return remote(
            chip.at[j, part(p)], up_buf.at[slot, part(p)], up_send.at[p, j], up_recv.at[p, slot], mate(j)
        )

    def chip_sum(s):
        j = (c + ORDER[s]) % PAIRS
        pair_copy(j).wait_recv()
        total = local[2 * j + e] + pair_buf[j]
        if ORDER[s]:
            chip[j] = total
            for p in range(2):
                up_copy(j, c, p).start()
        else:
            up_buf[c] = total

    for s in range(PAIRS):
        j = (c + ORDER[s]) % PAIRS
        load(0, k_hbm, k, j).wait()
        load(1, v_hbm, v, j).wait()
        sums = [None, None]
        for b in range(blocks):
            for half in range(2):
                at = (pl.ds(b * C, C), cols(2 * j + half, DH))
                own = lax.dot_general(k[at], v[at], (((0,), (0,)), ((), ())), preferred_element_type=F32)
                sums[half] = own if b == 0 else sums[half] + own
                if b + 1 < blocks:
                    low[2 * j + half, b] = sums[half].astype(BF16)
        local[2 * j] = sums[0]
        local[2 * j + 1] = sums[1]
        if s == 0:
            pl.semaphore_wait(barrier, expected)
        pair_copy(j).start()
        if s > 0:
            chip_sum(s - 1)
    for j in range(PAIRS):
        load(2, q_hbm, q, j).start()
    chip_sum(PAIRS - 1)
    whole_w = pltpu.make_async_copy(w_hbm, w, w_sem)
    whole_w.start()
    whole_gain = pltpu.make_async_copy(gain_hbm, gain, gain_sem)
    whole_gain.start()
    for j in range(PAIRS):
        load(2, q_hbm, q, j).wait()

    causal = lax.broadcasted_iota(jnp.int32, (C, C), 0) >= lax.broadcasted_iota(
        jnp.int32, (C, C), 1
    )

    def causal_part(h, _):
        left = []
        for b in range(blocks):
            at = (pl.ds(b * C, C), cols(h, DH))
            scores = lax.dot_general(q[at], k[at], (((1,), (1,)), ((), ())), preferred_element_type=F32)
            weights = jnp.where(causal, scores, 0.0).astype(BF16)
            left.append(jnp.concatenate([weights, q[at]], axis=1) if b else weights)
        for b in range(blocks):
            at = (pl.ds(b * C, C), cols(h, DH))
            right = jnp.concatenate([v[at], low[h, b - 1]], axis=0) if b else v[at]
            pre[at] = jnp.dot(left[b], right, preferred_element_type=F32)
        return 0

    done = 0

    def work(heads):
        nonlocal done
        until = min(H, done + heads)
        if until > done:
            lax.fori_loop(done, until, causal_part, 0)
        done = until

    def z_copy(d, target, p):
        return remote(zs.at[d, part(p)], zb.at[d, part(p)], z_send.at[p, d], z_recv.at[p, d], target)

    def z_start(d, p):
        @pl.when(group + (1 << d) < groups)
        def _():
            z_copy(d, me + (1 << d) * H, p).start()

    def z_take(d, p):
        rows = PARTS[p]

        @pl.when(group >= 1 << d)
        def _():
            z_copy(d, me - (1 << d) * H, p).wait_recv()
            zx[rows] = zx[rows] + zb[d, rows]

        if d + 1 < rounds:
            @pl.when(group >= 1 << d)
            def _():
                zs[d + 1, rows] = zs[d, rows] + zb[d, rows]

            @pl.when(group < 1 << d)
            def _():
                zs[d + 1, rows] = zs[d, rows]

    def down_copy(j, slot, p):
        return remote(
            down_src.at[j, part(p)], down_buf.at[slot, part(p)], down_send.at[p, j], down_recv.at[p, slot], mate(j)
        )

    def down_start(p):
        rows = PARTS[p]
        running = zx[rows]
        for i in range(PAIRS):
            down_src[i, rows] = running
            if i + 1 < PAIRS:
                running = running + up_buf[i, rows]
        for s in range(1, PAIRS):
            down_copy((c + s) % PAIRS, c, p).start()
        down_buf[c, rows] = down_src[c, rows]

    work(2)
    zx[...] = jnp.zeros_like(zx)
    for p in range(2):
        rows = PARTS[p]
        for s in range(1, PAIRS):
            j = (c + s) % PAIRS
            up_copy(j, j, p).wait_recv()
        zs[0, rows] = up_buf[0, rows] + up_buf[1, rows] + up_buf[2, rows] + up_buf[3, rows]
        z_start(0, p)
    work(2)
    for d in range(rounds):
        for p in range(2):
            z_take(d, p)
            if d + 1 < rounds:
                z_start(d + 1, p)
            else:
                down_start(p)
        if d + 1 < rounds:
            work(3)
    work(H)

    def fwd_copy(j, p):
        return remote(fwd.at[j, part(p)], pd.at[j, part(p)], fwd_send.at[p, j], fwd_recv.at[p, j], partner)

    def spread(s, p):
        j = (c + s) % PAIRS
        rows = PARTS[p]
        if s:
            down_copy(j, j, p).wait_recv()
        first = down_buf[j, rows]
        fwd[j, rows] = jnp.where(e == 0, first + local[2 * j, rows], first)
        fwd_copy(j, p).start()
        at = pl.ds(pl.multiple_of(e * DH + p * PART, PART), PART)
        half = pl.ds(pl.multiple_of(e * DH, DH), DH)
        diag[s, at, half] = jnp.where(e == 1, first + pair_buf[j, rows], first).astype(BF16)

    def norm(s):
        j = (c + s) % PAIRS
        for p in range(2):
            fwd_copy(j, p).wait_recv()
        half = pl.ds(pl.multiple_of((1 - e) * DH, DH), DH)
        diag[s, half, half] = pd[j].astype(BF16)
        carried = diag[s]
        for b in range(tok // CHUNK):
            at = (pl.ds(b * CHUNK, CHUNK), cols(j, PW))
            attended = pre[at] + jnp.dot(q[at], carried, preferred_element_type=F32)
            mean_square = jnp.dot((attended * attended).astype(BF16), averaging[...], preferred_element_type=F32)
            scaled = attended * lax.rsqrt(mean_square + 1e-06) * gain[:, cols(j, PW)]
            normed[at] = scaled.astype(BF16)

    whole_gain.wait()
    for s in range(PAIRS):
        spread(s, 0)
    spread(0, 1)
    for s in range(1, PAIRS):
        spread(s, 1)
        norm(s - 1)
    norm(PAIRS - 1)
    whole_w.wait()

    for s in range(PAIRS):
        j = (c + s) % PAIRS
        pair_copy(j).wait_send()
        for p in range(2):
            fwd_copy(j, p).wait_send()
            if s:
                up_copy(j, c, p).wait_send()
                down_copy(j, c, p).wait_send()
    for d in range(rounds):
        @pl.when(group + (1 << d) < groups)
        def _():
            for p in range(2):
                z_copy(d, me + (1 << d) * H, p).wait_send()


def scan_and_norm(n_outer, n_inner, queries, keys, values, norm_gain, out_weight):
    tok, width = queries.shape
    rounds = max(1, (n_outer * n_inner // H - 1).bit_length())
    state = lambda count: pltpu.VMEM((count, DH, DH), F32)
    sems = lambda *shape: pltpu.SemaphoreType.DMA(shape)
    whole = pltpu.VMEM((tok, width), BF16)
    vmem = pl.BlockSpec(memory_space=pltpu.VMEM)
    held = [pltpu.with_memory_space_constraint(x, pltpu.HBM) for x in (queries, keys, values, out_weight, norm_gain.reshape(1, width))]
    return pl.pallas_call(
        functools.partial(scan_kernel, n_outer, n_inner),
        out_shape=(
            jax.ShapeDtypeStruct((tok, width), BF16),
            jax.ShapeDtypeStruct(out_weight.shape, BF16),
        ),
        in_specs=[pl.BlockSpec(memory_space=pl.ANY)] * 5,
        out_specs=(vmem, vmem),
        scratch_shapes=[
            pltpu.VMEM((1, width), F32), whole, whole, whole, pltpu.VMEM((tok, width), F32),
            pltpu.VMEM((H, max(1, tok // C - 1), DH, DH), BF16), pltpu.VMEM((PAIRS, PW, PW), BF16),
            pltpu.VMEM((PW, PW), BF16), state(H), state(PAIRS), state(PAIRS), state(PAIRS),
            state(rounds), state(rounds), pltpu.VMEM((DH, DH), F32),
            state(PAIRS), state(PAIRS), state(PAIRS), state(PAIRS),
            sems(3, PAIRS), pltpu.SemaphoreType.DMA, pltpu.SemaphoreType.DMA, sems(PAIRS), sems(PAIRS), sems(2, PAIRS), sems(2, PAIRS),
            sems(2, rounds), sems(2, rounds), sems(2, PAIRS), sems(2, PAIRS), sems(2, PAIRS), sems(2, PAIRS),
        ],
        compiler_params=pltpu.CompilerParams(
            collective_id=0, has_side_effects=True, vmem_limit_bytes=32 * 1024 * 1024
        ),
        name="scan_and_norm",
    )(*held)


def project_kernel(normed, w, out_hbm, out, out_sem):
    tok, model = out.shape
    copies = []
    for r in range(tok // ROWS):
        for n in range(model // TILE):
            rows, at = pl.ds(r * ROWS, ROWS), pl.ds(n * TILE, TILE)
            out[rows, at] = jnp.dot(normed[rows, :], w[:, at], preferred_element_type=F32).astype(BF16)
            copy = pltpu.make_async_copy(out.at[rows, at], out_hbm.at[rows, at], out_sem.at[r, n])
            copy.start()
            copies.append(copy)
    for copy in copies:
        copy.wait()


def project(normed, out_weight):
    tok, model = normed.shape[0], out_weight.shape[1]
    return pl.pallas_call(
        project_kernel,
        out_shape=jax.ShapeDtypeStruct((tok, model), BF16),
        in_specs=[pl.BlockSpec(memory_space=pltpu.VMEM)] * 2,
        out_specs=pl.BlockSpec(memory_space=pl.ANY),
        scratch_shapes=[
            pltpu.VMEM((tok, model), BF16),
            pltpu.SemaphoreType.DMA((tok // ROWS, model // TILE)),
        ],
        compiler_params=pltpu.CompilerParams(vmem_limit_bytes=20 * 1024 * 1024),
        name="project",
    )(normed, out_weight)


def solution(mesh):
    n_outer, n_inner = mesh.shape["outer"], mesh.shape["inner"]

    def on_device(queries, keys, values, norm_gain, out_weight):
        normed, weight = scan_and_norm(n_outer, n_inner, queries, keys, values, norm_gain, out_weight)
        return project(normed, weight)

    rows = P(("outer", "inner"), None)
    return jax.shard_map(
        on_device,
        mesh=mesh,
        in_specs=(rows, rows, rows, P(), P()),
        out_specs=rows,
        check_vma=False,
    )
```
